128 devices in a mesh: views: 4 (over x), tiles: 32 (over z, y, core).
Axes of the slice: x: 4, y: 4, z: 4, core: 2. Of those that a mesh axis runs over, the one named last changes fastest.
Arguments:
- params: float32 [59, 65536], P(None, ('views', 'tiles')), as said below
- first_moment: float32 [59, 65536], P(None, ('views', 'tiles')), may hold values from -6 to 6
- second_moment: float32 [59, 65536], P(None, ('views', 'tiles')), may hold values from 0.5 to 20
- cameras: float32 [4, 6], replicated, may hold values from -0.02 to 0.02
- target: float32 [4, 512, 3, 256], P('views', 'tiles'), may hold values from 0 to 1
- lists: int32 [4, 512, 256], P('views', 'tiles'), may hold values from 0 to 65535, as said below
- lengths: int32 [4, 512], P('views', 'tiles'), may hold values from 32 to 256
Outputs:
- new_params: float32 [59, 65536], P(None, ('views', 'tiles'))
- new_first: float32 [59, 65536], P(None, ('views', 'tiles'))
- new_second: float32 [59, 65536], P(None, ('views', 'tiles'))
The draws below stay inside these ranges and needn't reach their ends.
Inputs may be any that keep to these rules, and one draw needn't show every extreme that they name: Each entry names a Gaussian by its column in params. The lists of the 16 tiles that one device holds (live entries or not) have exactly 32 entries in the columns of each device's shard of params. `params`: the quaternion's first entry is at least 0.6, the means lie in front of every camera, and the opacity logits are at most -2.
All inputs are finite; a program needn't handle non-finite values.
Results may differ from the reference program's by a relative error of at most 0.0003.
Values sent between devices are 32-bit elements; how exact they have to be, the bound alone decides.
No kernel may reach another device: no remote copies, remote signals or barrier semaphores. Data moves between devices by JAX's collectives and lax.ppermute only.
A program may use at most 128 MiB of HBM per device.

```python
import math
import jax
import jax.numpy as jnp
import numpy as np
from jax import lax

TILE_DEV = 16
LIST = 256
TILE_SIDE = 16
TILE_COLS = 32
PARAMS = 59
ADAM_STEP = 1000
G_DEV = 512
VIEWS = 4
TILES_VIEW = 512
GAUSS = 65536
PIXELS = 256


def draw_params(key, part):
    key = jax.random.fold_in(key, 11)
    key_list = jax.random.split(key, 9)
    width = TILE_COLS * TILE_SIDE
    height = TILES_VIEW // TILE_COLS * TILE_SIDE
    columns = jnp.arange(GAUSS, dtype=jnp.int32)
    home_tile = columns % G_DEV % TILES_VIEW
    screen_u = (home_tile % TILE_COLS * TILE_SIDE).astype(jnp.float32) + jax.random.uniform(key_list[0], (GAUSS,), jnp.float32, 0.0, float(TILE_SIDE))
    screen_v = (home_tile // TILE_COLS * TILE_SIDE).astype(jnp.float32) + jax.random.uniform(key_list[1], (GAUSS,), jnp.float32, 0.0, float(TILE_SIDE))
    depths = jax.random.uniform(key_list[2], (GAUSS,), jnp.float32, 4.0, 8.0)
    mean_x = (screen_u - 0.5 * width) * depths / width
    mean_y = (screen_v - 0.5 * height) * depths / width
    log_scale = jax.random.uniform(key_list[3], (3, GAUSS), jnp.float32, math.log(0.03), math.log(0.09))
    real_part = jax.random.uniform(key_list[4], (1, GAUSS), jnp.float32, 0.6, 1.0)
    imag_parts = jax.random.uniform(key_list[5], (3, GAUSS), jnp.float32, -0.4, 0.4)
    opacity_logit = jax.random.uniform(key_list[6], (1, GAUSS), jnp.float32, -4.5, -2.0)
    base_color = jax.random.uniform(key_list[7], (3, GAUSS), jnp.float32, -1.0, 1.0)
    higher = 0.25 * jax.random.normal(key_list[8], (45, GAUSS), jnp.float32)
    return jnp.concatenate([mean_x[None], mean_y[None], depths[None], log_scale, real_part, imag_parts, opacity_logit, base_color, higher], axis=0)


def draw_lists(key, part):
    key = jax.random.fold_in(key, 12)
    key_list = jax.random.split(key, 3)
    tile_rows = TILES_VIEW // TILE_COLS
    device_count = VIEWS * (TILES_VIEW // TILE_DEV)
    slot_count = TILE_DEV * LIST
    bucket = slot_count // device_count
    base = jnp.broadcast_to((jnp.arange(slot_count, dtype=jnp.int32) // bucket)[None, :], (device_count, slot_count))
    owners = jax.random.permutation(key_list[0], base, axis=1, independent=True).reshape(VIEWS, TILES_VIEW, LIST)
    shape_here = (VIEWS, TILES_VIEW, LIST)
    tile_ids = jnp.arange(TILES_VIEW, dtype=jnp.int32)[None, :, None]
    step_x = jax.random.randint(key_list[1], shape_here, -1, 2)
    step_y = jax.random.randint(key_list[2], shape_here, -1, 2)
    near_x = jnp.clip(tile_ids % TILE_COLS + step_x, 0, TILE_COLS - 1)
    near_y = jnp.clip(tile_ids // TILE_COLS + step_y, 0, tile_rows - 1)
    return (owners * G_DEV + (near_y * TILE_COLS + near_x) % G_DEV).astype(jnp.int32)


def draw_lengths(key, part):
    key = jax.random.fold_in(key, 13)
    tile_rows = TILES_VIEW // TILE_COLS
    tile_ids = jnp.arange(TILES_VIEW, dtype=jnp.int32)[None, :]
    row_of = tile_ids // TILE_COLS
    central = (row_of >= tile_rows // 4) & (row_of < tile_rows - tile_rows // 4)
    ceiling = jnp.where(central, LIST, LIST // 2)
    raw_draw = jax.random.randint(key, (VIEWS, TILES_VIEW), 0, LIST)
    drawn = LIST // 8 + raw_draw % (ceiling - LIST // 8 + 1)
    return jnp.where(central & (tile_ids % TILE_COLS == 0), LIST, drawn).astype(jnp.int32)


def block_levels(own_key, shape, cuts, low, top_value):
    loudness = 1.0
    for position, parts in cuts:
        heights = jax.random.uniform(jax.random.fold_in(jax.random.fold_in(own_key, 6), position), (parts,), jnp.float32, low / len(cuts), top_value / len(cuts))
        loudness = loudness * jnp.repeat(jnp.exp(heights), shape[position] // parts).reshape((-1,) + (1,) * (len(shape) - 1 - position))
    return loudness


def gaussian(rng, dims, spread, reach, pieces=(), held_as=jnp.bfloat16):
    values = spread * jax.random.normal(rng, dims, jnp.float32)
    if pieces:
        values = values * block_levels(rng, dims, pieces, -0.22, 0.18)
    return jnp.clip(values, -reach, reach).astype(held_as)


def setup_inputs(seed: int = 0) -> dict:
    keys = jax.random.split(jax.random.key(seed), 8)
    params = draw_params(jax.random.fold_in(keys[7], 71), 0)
    first_moment = gaussian(keys[1], (PARAMS, GAUSS), 1.0, 6.0, ((1, 128),), jnp.float32)
    second_moment = jnp.clip(jnp.exp(math.log(20.0) - 3.6888795 * jax.random.uniform(keys[2], (PARAMS, GAUSS), jnp.float32) ** block_levels(keys[2], (PARAMS, GAUSS), ((1, 128),), -0.2, 0.2)), 0.5, 20.0)
    cameras = jnp.clip(jax.random.uniform(keys[3], (VIEWS, 6), jnp.float32, -0.02, 0.02), -0.02, 0.02)
    target = jnp.clip(1.0 * jax.random.uniform(keys[4], (VIEWS, TILES_VIEW, 3, PIXELS), jnp.float32) ** block_levels(keys[4], (VIEWS, TILES_VIEW, 3, PIXELS), ((0, 4), (1, 32)), -0.2, 0.2), 0.0, 1.0)
    lists = draw_lists(jax.random.fold_in(keys[7], 71), 0)
    lengths = draw_lengths(jax.random.fold_in(keys[7], 71), 0)
    return dict(params=params, first_moment=first_moment, second_moment=second_moment, cameras=cameras, target=target, lists=lists, lengths=lengths)


sh_zero = 0.28209479177387814
sh_first = 0.4886025119029199
sh_second = (1.0925484305920792, -1.0925484305920792, 0.31539156525252005, -1.0925484305920792, 0.5462742152960396)
sh_third = (-0.5900435899266435, 2.890611442640554, -0.4570457994644658, 0.3731763325901154, -0.4570457994644658, 1.445305721320277, -0.5900435899266435)
beta_one = 0.9
beta_two = 0.999
adam_eps = 1e-15
learning = np.concatenate([np.full(3, 0.00016), np.full(3, 0.005), np.full(4, 0.001), np.full(1, 0.05), np.full(3, 0.0025), np.full(45, 0.000125)]).astype(np.float32)[:, None]

def matmul_three(left, right):
    return [[left[row_at][0] * right[0][col_at] + left[row_at][1] * right[1][col_at] + left[row_at][2] * right[2][col_at] for col_at in range(3)] for row_at in range(3)]

def camera_rotation(camera):
    cos_a, sin_a = (jnp.cos(camera[0]), jnp.sin(camera[0]))
    cos_b, sin_b = (jnp.cos(camera[1]), jnp.sin(camera[1]))
    cos_c, sin_c = (jnp.cos(camera[2]), jnp.sin(camera[2]))
    around_x = [[1.0, 0.0, 0.0], [0.0, cos_a, -sin_a], [0.0, sin_a, cos_a]]
    around_y = [[cos_b, 0.0, sin_b], [0.0, 1.0, 0.0], [-sin_b, 0.0, cos_b]]
    around_z = [[cos_c, -sin_c, 0.0], [sin_c, cos_c, 0.0], [0.0, 0.0, 1.0]]
    return matmul_three(around_z, matmul_three(around_y, around_x))

def sh_basis(along_x, along_y, along_z):
    square_x, square_y, square_z = (along_x * along_x, along_y * along_y, along_z * along_z)
    both_xy, both_yz, both_xz = (along_x * along_y, along_y * along_z, along_x * along_z)
    return [sh_zero + 0.0 * along_x, -sh_first * along_y, sh_first * along_z, -sh_first * along_x, sh_second[0] * both_xy, sh_second[1] * both_yz, sh_second[2] * (2.0 * square_z - square_x - square_y), sh_second[3] * both_xz, sh_second[4] * (square_x - square_y), sh_third[0] * along_y * (3.0 * square_x - square_y), sh_third[1] * both_xy * along_z, sh_third[2] * along_y * (4.0 * square_z - square_x - square_y), sh_third[3] * along_z * (2.0 * square_z - 3.0 * square_x - 3.0 * square_y), sh_third[4] * along_x * (4.0 * square_z - square_x - square_y), sh_third[5] * along_z * (square_x - square_y), sh_third[6] * along_x * (square_x - 3.0 * square_y)]

def project(params, camera, focal_len, center_x, center_y):
    rotation = camera_rotation(camera)
    means = [params[0], params[1], params[2]]
    point = [rotation[axis_at][0] * means[0] + rotation[axis_at][1] * means[1] + rotation[axis_at][2] * means[2] + camera[3 + axis_at] for axis_at in range(3)]
    inverse_z = 1.0 / point[2]
    screen_u = focal_len * point[0] * inverse_z + center_x
    screen_v = focal_len * point[1] * inverse_z + center_y
    scales = jnp.exp(params[3:6])
    unit_quat = params[6:10] * lax.rsqrt(lax.optimization_barrier(jnp.sum(params[6:10] * params[6:10], axis=0)))
    real_part, imag_x, imag_y, imag_z = (unit_quat[0], unit_quat[1], unit_quat[2], unit_quat[3])
    spin = [[1.0 - 2.0 * (imag_y * imag_y + imag_z * imag_z), 2.0 * (imag_x * imag_y - real_part * imag_z), 2.0 * (imag_x * imag_z + real_part * imag_y)], [2.0 * (imag_x * imag_y + real_part * imag_z), 1.0 - 2.0 * (imag_x * imag_x + imag_z * imag_z), 2.0 * (imag_y * imag_z - real_part * imag_x)], [2.0 * (imag_x * imag_z - real_part * imag_y), 2.0 * (imag_y * imag_z + real_part * imag_x), 1.0 - 2.0 * (imag_x * imag_x + imag_y * imag_y)]]
    turned = matmul_three(rotation, spin)
    shaped = [[turned[row_at][col_at] * scales[col_at] for col_at in range(3)] for row_at in range(3)]
    near_x = [focal_len * inverse_z * shaped[0][col_at] - focal_len * point[0] * inverse_z * inverse_z * shaped[2][col_at] for col_at in range(3)]
    near_y = [focal_len * inverse_z * shaped[1][col_at] - focal_len * point[1] * inverse_z * inverse_z * shaped[2][col_at] for col_at in range(3)]
    cov_a = near_x[0] * near_x[0] + near_x[1] * near_x[1] + near_x[2] * near_x[2] + 0.3
    cov_b = near_x[0] * near_y[0] + near_x[1] * near_y[1] + near_x[2] * near_y[2]
    cov_c = near_y[0] * near_y[0] + near_y[1] * near_y[1] + near_y[2] * near_y[2] + 0.3
    determinant = cov_a * cov_c - cov_b * cov_b
    offset = [means[axis_at] + rotation[0][axis_at] * camera[3] + rotation[1][axis_at] * camera[4] + rotation[2][axis_at] * camera[5] for axis_at in range(3)]
    inverse_len = lax.rsqrt(offset[0] * offset[0] + offset[1] * offset[1] + offset[2] * offset[2])
    basis = sh_basis(offset[0] * inverse_len, offset[1] * inverse_len, offset[2] * inverse_len)
    colors = [0.5 + sum((basis[coef_at] * params[11 + 3 * coef_at + channel] for coef_at in range(16))) for channel in range(3)]
    opacity = jax.nn.sigmoid(params[10])
    return jnp.stack([screen_u, screen_v, cov_c / determinant, -cov_b / determinant, cov_a / determinant, opacity, colors[0], colors[1], colors[2]])

def composite(picked, lengths, target, first_tile):
    tile_count = picked.shape[1]
    list_size = picked.shape[2]
    tile_ids = first_tile + jnp.arange(tile_count, dtype=jnp.int32)
    pixel_ids = jnp.arange(TILE_SIDE * TILE_SIDE, dtype=jnp.int32)
    pixel_x = (tile_ids % TILE_COLS * TILE_SIDE)[:, None] + (pixel_ids % TILE_SIDE)[None, :]
    pixel_y = (tile_ids // TILE_COLS * TILE_SIDE)[:, None] + (pixel_ids // TILE_SIDE)[None, :]
    delta_x = pixel_x.astype(jnp.float32)[:, None, :] + 0.5 - picked[0][:, :, None]
    delta_y = pixel_y.astype(jnp.float32)[:, None, :] + 0.5 - picked[1][:, :, None]
    quadric = picked[2][:, :, None] * delta_x * delta_x + 2.0 * picked[3][:, :, None] * delta_x * delta_y + picked[4][:, :, None] * delta_y * delta_y
    live_mask = jnp.arange(list_size, dtype=jnp.int32)[None, :] < lengths[:, None]
    alphas = jnp.where(live_mask[:, :, None], picked[5][:, :, None] * jnp.exp(-0.5 * quadric), 0.0)
    log_keep = jnp.log1p(-alphas)
    weight = jnp.exp(jnp.cumsum(log_keep, axis=1) - log_keep) * alphas
    render = jnp.stack([lax.optimization_barrier(jnp.sum(weight * picked[6 + channel][:, :, None], axis=1)) for channel in range(3)], axis=1)
    return jnp.sum(jnp.abs(render - target))

def adam_update(params, first_moment, second_moment, gradient):
    new_first = beta_one * first_moment + (1.0 - beta_one) * gradient
    new_second = beta_two * second_moment + (1.0 - beta_two) * gradient * gradient
    step_size = learning * (new_first / (1.0 - beta_one ** ADAM_STEP))
    new_params = params - step_size / (jnp.sqrt(new_second / (1.0 - beta_two ** ADAM_STEP)) + adam_eps)
    return (new_params, new_first, new_second)

def view_gradient(projected, lists, lengths, target):
    tile_rows = lists.shape[0] // TILE_COLS
    blocks = (lists.reshape(tile_rows, TILE_COLS, -1), lengths.reshape(tile_rows, TILE_COLS), target.reshape(tile_rows, TILE_COLS, 3, -1), jnp.arange(tile_rows, dtype=jnp.int32) * TILE_COLS)

    def one_block(dense_rows, block):
        indices, block_len, block_target, first_tile = block
        picked = jnp.take(projected, indices, axis=1)
        _, pull_block = jax.vjp(lambda chosen: composite(chosen, block_len, block_target, first_tile), picked)
        picked_grad = pull_block(jnp.ones((), projected.dtype))[0]
        dense_rows = dense_rows.at[:, indices.reshape(-1)].add(picked_grad.reshape(projected.shape[0], -1))
        return (dense_rows, None)
    dense_rows, _ = lax.scan(one_block, jnp.zeros_like(projected), blocks)
    return dense_rows

def reference(params, first_moment, second_moment, cameras, target, lists, lengths):
    width = TILE_COLS * TILE_SIDE
    height = TILES_VIEW // TILE_COLS * TILE_SIDE
    focal_len = float(width)

    def all_views(values):
        return jnp.stack([project(values, cameras[camera_at], focal_len, 0.5 * width, 0.5 * height) for camera_at in range(VIEWS)])
    projected, pullback = jax.vjp(all_views, params)
    row_grads = jnp.stack([view_gradient(projected[camera_at], lists[camera_at], lengths[camera_at], target[camera_at]) for camera_at in range(VIEWS)])
    gradient = pullback(row_grads)[0]
    return adam_update(params, first_moment, second_moment, gradient)
```

```python
import jax
import jax.numpy as jnp
import numpy as np
from jax import lax
from jax.experimental import pallas as pl
from jax.experimental.pallas import tpu as pltpu
from jax.sharding import PartitionSpec as P

TILE_SIDE = 16
TILE_COLS = 32
ADAM_STEP = 1000
GROUP = 8
LANES = 128
VIEWS = 4
SLOTS = 32
FEATURES = 9
AXES = ("views", "tiles")

f32 = jnp.float32
bf16 = jnp.bfloat16
i32 = jnp.int32

sh_zero = 0.28209479177387814
sh_first = 0.4886025119029199
sh_second = (
    1.0925484305920792,
    -1.0925484305920792,
    0.31539156525252005,
    -1.0925484305920792,
    0.5462742152960396,
)
sh_third = (
    -0.5900435899266435,
    2.890611442640554,
    -0.4570457994644658,
    0.3731763325901154,
    -0.4570457994644658,
    1.445305721320277,
    -0.5900435899266435,
)
beta_one = 0.9
beta_two = 0.999
adam_eps = 1e-15


def matmul_three(left, right):
    return [
        [
            left[row_at][0] * right[0][col_at]
            + left[row_at][1] * right[1][col_at]
            + left[row_at][2] * right[2][col_at]
            for col_at in range(3)
        ]
        for row_at in range(3)
    ]


def rotation_entries(cos, sin):
    cos_a, cos_b, cos_c = cos
    sin_a, sin_b, sin_c = sin
    return [
        [cos_c * cos_b, cos_c * sin_b * sin_a - sin_c * cos_a, cos_c * sin_b * cos_a + sin_c * sin_a],
        [sin_c * cos_b, sin_c * sin_b * sin_a + cos_c * cos_a, sin_c * sin_b * cos_a - cos_c * sin_a],
        [-sin_b, cos_b * sin_a, cos_b * cos_a],
    ]


def sh_basis(along_x, along_y, along_z):
    square_x, square_y, square_z = (along_x * along_x, along_y * along_y, along_z * along_z)
    both_xy, both_yz, both_xz = (along_x * along_y, along_y * along_z, along_x * along_z)
    return [
        sh_zero + 0.0 * along_x,
        -sh_first * along_y,
        sh_first * along_z,
        -sh_first * along_x,
        sh_second[0] * both_xy,
        sh_second[1] * both_yz,
        sh_second[2] * (2.0 * square_z - square_x - square_y),
        sh_second[3] * both_xz,
        sh_second[4] * (square_x - square_y),
        sh_third[0] * along_y * (3.0 * square_x - square_y),
        sh_third[1] * both_xy * along_z,
        sh_third[2] * along_y * (4.0 * square_z - square_x - square_y),
        sh_third[3] * along_z * (2.0 * square_z - 3.0 * square_x - 3.0 * square_y),
        sh_third[4] * along_x * (4.0 * square_z - square_x - square_y),
        sh_third[5] * along_z * (square_x - square_y),
        sh_third[6] * along_x * (square_x - 3.0 * square_y),
    ]


def project(params, rotation, shift, focal_len, center_x, center_y):
    means = params[:3]
    point = [
        rotation[axis_at][0] * means[0]
        + rotation[axis_at][1] * means[1]
        + rotation[axis_at][2] * means[2]
        + shift[axis_at]
        for axis_at in range(3)
    ]
    inverse_z = 1.0 / point[2]
    screen_u = focal_len * point[0] * inverse_z + center_x
    screen_v = focal_len * point[1] * inverse_z + center_y
    scales = [jnp.exp(params[3 + axis_at]) for axis_at in range(3)]
    quat = params[6:10]
    inverse_norm = lax.rsqrt(
        quat[0] * quat[0] + quat[1] * quat[1] + quat[2] * quat[2] + quat[3] * quat[3]
    )
    real_part, imag_x, imag_y, imag_z = [part * inverse_norm for part in quat]
    spin = [
        [
            1.0 - 2.0 * (imag_y * imag_y + imag_z * imag_z),
            2.0 * (imag_x * imag_y - real_part * imag_z),
            2.0 * (imag_x * imag_z + real_part * imag_y),
        ],
        [
            2.0 * (imag_x * imag_y + real_part * imag_z),
            1.0 - 2.0 * (imag_x * imag_x + imag_z * imag_z),
            2.0 * (imag_y * imag_z - real_part * imag_x),
        ],
        [
            2.0 * (imag_x * imag_z - real_part * imag_y),
            2.0 * (imag_y * imag_z + real_part * imag_x),
            1.0 - 2.0 * (imag_x * imag_x + imag_y * imag_y),
        ],
    ]
    turned = matmul_three(rotation, spin)
    shaped = [
        [turned[row_at][col_at] * scales[col_at] for col_at in range(3)] for row_at in range(3)
    ]
    near_x = [
        focal_len * inverse_z * shaped[0][col_at]
        - focal_len * point[0] * inverse_z * inverse_z * shaped[2][col_at]
        for col_at in range(3)
    ]
    near_y = [
        focal_len * inverse_z * shaped[1][col_at]
        - focal_len * point[1] * inverse_z * inverse_z * shaped[2][col_at]
        for col_at in range(3)
    ]
    cov_a = near_x[0] * near_x[0] + near_x[1] * near_x[1] + near_x[2] * near_x[2] + 0.3
    cov_b = near_x[0] * near_y[0] + near_x[1] * near_y[1] + near_x[2] * near_y[2]
    cov_c = near_y[0] * near_y[0] + near_y[1] * near_y[1] + near_y[2] * near_y[2] + 0.3
    determinant = cov_a * cov_c - cov_b * cov_b
    offset = [
        means[axis_at]
        + rotation[0][axis_at] * shift[0]
        + rotation[1][axis_at] * shift[1]
        + rotation[2][axis_at] * shift[2]
        for axis_at in range(3)
    ]
    inverse_len = lax.rsqrt(offset[0] * offset[0] + offset[1] * offset[1] + offset[2] * offset[2])
    basis = sh_basis(offset[0] * inverse_len, offset[1] * inverse_len, offset[2] * inverse_len)
    colors = [
        0.5 + sum((basis[coef_at] * params[11 + 3 * coef_at + channel] for coef_at in range(16)))
        for channel in range(3)
    ]
    log_opacity = params[10] - jnp.log1p(jnp.exp(params[10]))
    return [
        screen_u,
        screen_v,
        cov_c / determinant,
        -cov_b / determinant,
        cov_a / determinant,
        log_opacity,
        colors[0],
        colors[1],
        colors[2],
    ]


def camera_terms(cameras_ref, owned):
    cameras = cameras_ref[...]
    cos, sin = jnp.cos(cameras), jnp.sin(cameras)

    def column(values, at):
        return jnp.broadcast_to(values[:, at : at + 1], (VIEWS, owned))

    rotation = rotation_entries(
        [column(cos, at) for at in range(3)], [column(sin, at) for at in range(3)]
    )
    return rotation, [column(cameras, 3 + at) for at in range(3)]


def iota(shape, dim):
    return lax.broadcasted_iota(i32, shape, dim)


def dot(left, right, left_dim, right_dim):
    return lax.dot_general(
        left, right, (((left_dim,), (right_dim,)), ((), ())), preferred_element_type=f32
    )


def pieces(values, count):
    out = []
    for at in range(count):
        part = values.astype(bf16)
        out.append(part)
        if at + 1 < count:
            values = values - part.astype(f32)
    return out


def rank_kernel(owned, entries_ref, rank_ref, request_ref):
    chunks = entries_ref.shape[0]
    entries = entries_ref[...]
    owner = lax.rem(lax.div(entries, owned), LANES)
    column = lax.rem(entries, owned)
    low = lax.rem(column, 256).astype(f32)
    high = lax.div(column, 256).astype(f32)
    before = jnp.where(iota((LANES, LANES), 0) < iota((LANES, LANES), 1), 1.0, 0.0)
    adder = jnp.concatenate([before, jnp.ones((LANES, LANES), f32)], axis=1).astype(bf16)
    owner_id = iota((LANES, LANES), 0)
    slot_id = iota((SLOTS, LANES), 0)
    base = jnp.zeros((LANES, LANES), f32)
    requests = jnp.zeros((LANES, 2 * SLOTS), f32)
    for at in range(chunks):
        hot = owner_id == owner[at : at + 1, :]
        hot_one = jnp.where(hot, 1.0, 0.0).astype(bf16)
        counts = dot(hot_one, adder, 1, 0)
        rank = jnp.sum(
            jnp.where(hot, counts[:, :LANES] + base, 0.0), axis=0, keepdims=True
        ).astype(i32)
        base = base + counts[:, LANES:]
        rank_ref[at : at + 1, :] = rank
        slot = slot_id == rank
        wanted = jnp.concatenate(
            [
                jnp.where(slot, low[at : at + 1, :], 0.0),
                jnp.where(slot, high[at : at + 1, :], 0.0),
            ],
            axis=0,
        ).astype(bf16)
        requests = requests + dot(hot_one, wanted, 1, 1)
    request_ref[...] = requests[:, :SLOTS] + 256.0 * requests[:, SLOTS:]


def flipped_requests(asked_ref):
    asked = asked_ref[...]
    wide = jnp.concatenate([asked, jnp.zeros((LANES, LANES - SLOTS), f32)], axis=1)
    return wide.T[:SLOTS, :].astype(i32)


def answer_kernel(frame, params_ref, cameras_ref, asked_ref, rows_ref):
    owned = params_ref.shape[1]
    rotation, shift = camera_terms(cameras_ref, owned)
    params = [jnp.broadcast_to(params_ref[at : at + 1, :], (VIEWS, owned)) for at in range(59)]
    projected = project(params, rotation, shift, *frame)
    asked = flipped_requests(asked_ref)
    chunk_of = lax.div(asked, LANES)
    lane_of = lax.rem(asked, LANES)
    view_of = lax.div(iota((SLOTS, LANES), 1), LANES // VIEWS)
    chosen = [jnp.zeros((SLOTS, LANES), f32) for _ in range(FEATURES)]
    for view in range(VIEWS):
        for chunk in range(owned // LANES):
            mask = (view_of == view) & (chunk_of == chunk)
            for at in range(FEATURES):
                source = jnp.broadcast_to(
                    projected[at][view : view + 1, chunk * LANES : (chunk + 1) * LANES],
                    (SLOTS, LANES),
                )
                found = jnp.take_along_axis(source, lane_of, axis=1, mode="promise_in_bounds")
                chosen[at] = jnp.where(mask, found, chosen[at])
    for part in range(3):
        stack = chosen[4 * part : 4 * part + 4]
        while len(stack) < 4:
            stack.append(jnp.zeros((SLOTS, LANES), f32))
        rows_ref[:, part * LANES : (part + 1) * LANES] = jnp.concatenate(stack, axis=0).T


def tile_kernel(
    owned,
    entries_ref,
    rank_ref,
    rows_ref,
    target_ref,
    grads_ref,
    source_ref,
    coef_ref,
    color_ref,
    alpha_ref,
    weight_ref,
    moment_ref,
    grad_ref,
):
    chunks = entries_ref.shape[0]
    groups = 2
    per_group = chunks // groups
    pixels = TILE_SIDE * TILE_SIDE
    steps = LANES // GROUP
    first_tile = lax.axis_index("tiles") * (groups * GROUP)

    for part in range(3):
        source_ref[part * LANES : (part + 1) * LANES, :] = rows_ref[
            :, part * LANES : (part + 1) * LANES
        ].T
    entries = entries_ref[...]
    owner = lax.rem(lax.div(entries, owned), LANES)
    live = entries < owned * LANES
    rank = rank_ref[...]
    shape = (chunks, LANES)
    chosen = [jnp.zeros(shape, f32) for _ in range(FEATURES)]
    for slot in range(SLOTS):
        mask = rank == slot
        for at in range(FEATURES):
            row = at * SLOTS + slot
            source = jnp.broadcast_to(source_ref[row : row + 1, :], shape)
            found = jnp.take_along_axis(source, owner, axis=1, mode="promise_in_bounds")
            chosen[at] = jnp.where(mask, found, chosen[at])

    tile = first_tile + lax.div(iota(shape, 0), per_group) * GROUP + lax.rem(iota(shape, 1), GROUP)
    middle_x = (lax.rem(tile, TILE_COLS) * TILE_SIDE + TILE_SIDE // 2).astype(f32)
    middle_y = (lax.div(tile, TILE_COLS) * TILE_SIDE + TILE_SIDE // 2).astype(f32)
    at_u = chosen[0] - middle_x
    at_v = chosen[1] - middle_y
    conic_a, conic_b, conic_c = chosen[2], chosen[3], chosen[4]
    by_u = conic_a * at_u + conic_b * at_v
    by_v = conic_b * at_u + conic_c * at_v
    coefs = [
        jnp.where(live, chosen[5] - 0.5 * (at_u * by_u + at_v * by_v), -1e4),
        jnp.where(live, by_u, 0.0),
        jnp.where(live, by_v, 0.0),
        jnp.where(live, -0.5 * conic_a, 0.0),
        jnp.where(live, -conic_b, 0.0),
        jnp.where(live, -0.5 * conic_c, 0.0),
    ]
    for at in range(8):
        split = pieces(coefs[at], 3) if at < 6 else [jnp.zeros(shape, bf16)] * 3
        for part in range(3):
            row = (part * 8 + at) * chunks
            coef_ref[row : row + chunks, :] = split[part].astype(f32)
    for at in range(3):
        split = pieces(chosen[6 + at], 3)
        for part in range(3):
            row = (part * 3 + at) * chunks
            color_ref[row : row + chunks, :] = split[part].astype(f32)

    pixel = iota((8, pixels), 1)
    row8 = iota((8, pixels), 0)
    off_x = lax.rem(pixel, TILE_SIDE).astype(f32) - 7.5
    off_y = lax.div(pixel, TILE_SIDE).astype(f32) - 7.5
    base = jnp.where(row8 == 0, 1.0, 0.0)
    for at, values in enumerate([off_x, off_y, off_x * off_x, off_x * off_y, off_y * off_y]):
        base = jnp.where(row8 == at + 1, values, base)
    base_one = base.astype(bf16)
    base_three = jnp.concatenate([base, base, base], axis=0).astype(bf16)
    same_tile = lax.rem(iota((GROUP, LANES), 1), GROUP) == iota((GROUP, LANES), 0)

    def color_rows(chunk):
        rows = []
        for part in range(9):
            row = color_ref[pl.ds(part * chunks + chunk, 1), :]
            rows.append(jnp.where(same_tile, jnp.broadcast_to(row, (GROUP, LANES)), 0.0))
        return jnp.concatenate(rows, axis=0).astype(bf16)

    def forward(at, carry):
        out = []
        for group in range(groups):
            clear, render = carry[group]
            chunk = group * per_group + at
            coef = coef_ref[pl.ds(chunk, 24, stride=chunks), :].astype(bf16)
            alpha = jnp.exp(dot(coef, base_three, 0, 0))
            start = pl.multiple_of(chunk * LANES, LANES)
            alpha_ref[pl.ds(start, LANES), :] = alpha
            weights = []
            for step in range(steps):
                weight = alpha[step * GROUP : (step + 1) * GROUP, :] * clear
                clear = clear - weight
                weights.append(weight)
            weight = jnp.concatenate(weights, axis=0)
            weight_ref[pl.ds(start, LANES), :] = weight
            colors = color_rows(chunk)
            high, middle, low = pieces(weight, 3)
            render = render + (
                dot(colors, high, 1, 0)
                + jnp.concatenate(
                    [dot(colors[:48], middle, 1, 0), jnp.zeros((24, pixels), f32)], axis=0
                )
            )
            render = render + jnp.concatenate(
                [dot(colors[:24], low, 1, 0), jnp.zeros((48, pixels), f32)], axis=0
            )
            out.append((clear, render))
        return tuple(out)

    start_state = (jnp.ones((GROUP, pixels), f32), jnp.zeros((72, pixels), f32))
    done = lax.fori_loop(0, per_group, forward, (start_state,) * groups)

    signs = []
    for group in range(groups):
        render = done[group][1]
        render = render[:24] + (render[24:48] + render[48:])
        rows = []
        for at in range(3):
            gap = (
                render[at * GROUP : (at + 1) * GROUP, :]
                - target_ref[group * GROUP : (group + 1) * GROUP, at, :]
            )
            rows.append(jnp.where(gap > 0.0, 1.0, jnp.where(gap < 0.0, -1.0, 0.0)))
        signs.append(jnp.concatenate(rows, axis=0))

    def backward(back, carry):
        at = per_group - 1 - back
        out = []
        for group in range(groups):
            behind = carry[group]
            chunk = group * per_group + at
            start = pl.multiple_of(chunk * LANES, LANES)
            sign = signs[group].astype(bf16)
            sign_three = jnp.concatenate([signs[group]] * 3, axis=0).astype(bf16)
            pull = dot(color_rows(chunk), sign_three, 0, 0)
            alpha = alpha_ref[pl.ds(start, LANES), :]
            weight = weight_ref[pl.ds(start, LANES), :]
            by_alpha = [None] * steps
            for step in reversed(range(steps)):
                rows = slice(step * GROUP, (step + 1) * GROUP)
                gap = pull[rows, :] - behind
                by_alpha[step] = weight[rows, :] * gap
                behind = behind + alpha[rows, :] * gap
            high, low = pieces(jnp.concatenate(by_alpha, axis=0), 2)
            moments = dot(base_one, high, 1, 1) + dot(base_one, low, 1, 1)
            high, low = pieces(weight, 2)
            by_color = dot(sign, high, 1, 1) + dot(sign, low, 1, 1)
            row = pl.multiple_of(chunk * 16, 16)
            moment_ref[pl.ds(row, 8), :] = moments
            for channel in range(3):
                moment_ref[pl.ds(row + 8 + channel, 1), :] = jnp.sum(
                    jnp.where(same_tile, by_color[channel * GROUP : (channel + 1) * GROUP], 0.0),
                    axis=0,
                    keepdims=True,
                )
            out.append(behind)
        return tuple(out)

    lax.fori_loop(0, per_group, backward, (jnp.zeros((GROUP, pixels), f32),) * groups)

    sums = [moment_ref[pl.ds(at, chunks, stride=16), :] for at in range(6)]
    sum_x = sums[1] - at_u * sums[0]
    sum_y = sums[2] - at_v * sums[0]
    sum_xx = sums[3] - 2.0 * at_u * sums[1] + at_u * at_u * sums[0]
    sum_xy = sums[4] - at_u * sums[2] - at_v * sum_x
    sum_yy = sums[5] - 2.0 * at_v * sums[2] + at_v * at_v * sums[0]
    grads = [
        conic_a * sum_x + conic_b * sum_y,
        conic_b * sum_x + conic_c * sum_y,
        -0.5 * sum_xx,
        -sum_xy,
        -0.5 * sum_yy,
        sums[0],
    ] + [moment_ref[pl.ds(8 + at, chunks, stride=16), :] for at in range(3)]
    for at in range(FEATURES):
        grad_ref[at * chunks : (at + 1) * chunks, :] = jnp.where(live, grads[at], 0.0)

    owner_id = iota((LANES, LANES), 0)
    slot_id = iota((SLOTS, LANES), 0)

    def scatter(chunk, total):
        own = lax.rem(lax.div(entries_ref[pl.ds(chunk, 1), :], owned), LANES)
        hot = jnp.where(owner_id == own, 1.0, 0.0).astype(bf16)
        slot = slot_id == rank_ref[pl.ds(chunk, 1), :]
        rows = []
        for at in range(FEATURES):
            row = grad_ref[pl.ds(at * chunks + chunk, 1), :]
            rows.append(jnp.where(slot, jnp.broadcast_to(row, (SLOTS, LANES)), 0.0))
        high, low = pieces(jnp.concatenate(rows, axis=0), 2)
        return total + (dot(hot, high, 1, 1) + dot(hot, low, 1, 1))

    total = lax.fori_loop(0, chunks, scatter, jnp.zeros((LANES, FEATURES * SLOTS), f32))
    grads_ref[...] = jnp.concatenate(
        [total, jnp.zeros((LANES, 3 * LANES - FEATURES * SLOTS), f32)], axis=1
    )


def update_kernel(
    frame,
    params_ref,
    first_ref,
    second_ref,
    cameras_ref,
    asked_ref,
    grads_ref,
    rates_ref,
    new_params_ref,
    new_first_ref,
    new_second_ref,
    source_ref,
    dense_ref,
    gradient_ref,
):
    owned = params_ref.shape[1]
    asked = flipped_requests(asked_ref)
    for part in range(3):
        source_ref[part * LANES : (part + 1) * LANES, :] = grads_ref[
            :, part * LANES : (part + 1) * LANES
        ].T
    source_ref[3 * LANES :, :] = jnp.zeros((LANES, LANES), f32)
    view_of = lax.div(iota((16, LANES), 1), LANES // VIEWS)
    column_id = iota((owned, LANES), 0)
    dense = jnp.zeros((2 * VIEWS * 16, owned), f32)
    for slot in range(SLOTS):
        hot = jnp.where(column_id == asked[slot : slot + 1, :], 1.0, 0.0).astype(bf16)
        values = source_ref[pl.ds(slot, 16, stride=SLOTS), :]
        values = jnp.concatenate(
            [jnp.where(view_of == view, values, 0.0) for view in range(VIEWS)], axis=0
        )
        high, low = pieces(values, 2)
        dense = dense + dot(jnp.concatenate([high, low], axis=0), hot, 1, 1)
    dense = dense[: VIEWS * 16] + dense[VIEWS * 16 :]
    spans = range(owned // LANES)
    for span in spans:
        dense_ref[span * VIEWS * 16 : (span + 1) * VIEWS * 16, :] = dense[
            :, span * LANES : (span + 1) * LANES
        ]
    cotangents = [
        jnp.concatenate(
            [dense_ref[pl.ds(span * VIEWS * 16 + at, VIEWS, stride=16), :] for span in spans], axis=1
        )
        for at in range(FEATURES)
    ]

    rotation, shift = camera_terms(cameras_ref, owned)
    params = [jnp.broadcast_to(params_ref[at : at + 1, :], (VIEWS, owned)) for at in range(59)]
    _, pullback = jax.vjp(lambda values: project(values, rotation, shift, *frame), params)
    by_params = pullback(cotangents)[0]
    for at in range(59):
        gradient_ref[at : at + 1, :] = jnp.sum(by_params[at], axis=0, keepdims=True)
    gradient = gradient_ref[:59, :]
    new_first = beta_one * first_ref[...] + (1.0 - beta_one) * gradient
    new_second = beta_two * second_ref[...] + (1.0 - beta_two) * gradient * gradient
    new_first_ref[...] = new_first
    new_second_ref[...] = new_second
    step_size = rates_ref[...] * (new_first / (1.0 - beta_one**ADAM_STEP))
    new_params_ref[...] = params_ref[...] - step_size / (
        jnp.sqrt(new_second / (1.0 - beta_two**ADAM_STEP)) + adam_eps
    )


learning = np.concatenate(
    [
        np.full(3, 0.00016),
        np.full(3, 0.005),
        np.full(4, 0.001),
        np.full(1, 0.05),
        np.full(3, 0.0025),
        np.full(45, 0.000125),
    ]
).astype(np.float32)[:, None]


def per_device(params, first_moment, second_moment, cameras, target, lists, lengths):
    owned = params.shape[1]
    list_size = lists.shape[2]
    tile_dev = lists.shape[1]
    entry_count = tile_dev * list_size
    chunks = entry_count // LANES
    width = TILE_COLS * TILE_SIDE
    height = tile_dev * lax.axis_size("tiles") // TILE_COLS * TILE_SIDE
    frame = (float(width), 0.5 * width, 0.5 * height)
    limits = pltpu.CompilerParams(vmem_limit_bytes=48 * 1024 * 1024)

    dead = jnp.arange(list_size, dtype=i32)[None, :] >= lengths[0][:, None]
    entries = lists[0] + jnp.where(dead, owned * LANES, 0)
    entries = (
        entries.reshape(tile_dev // GROUP, GROUP, list_size).transpose(0, 2, 1).reshape(chunks, LANES)
    )

    def full(shape, dtype=f32):
        return jax.ShapeDtypeStruct(shape, dtype)

    rank, requests = pl.pallas_call(
        lambda *refs: rank_kernel(owned, *refs),
        out_shape=(full((chunks, LANES), i32), full((LANES, SLOTS))),
        compiler_params=limits,
        name="rank",
    )(entries)
    asked = lax.all_to_all(requests, AXES, 0, 0, tiled=True)
    answers = pl.pallas_call(
        lambda *refs: answer_kernel(frame, *refs),
        out_shape=full((LANES, 3 * LANES)),
        compiler_params=limits,
        name="answer",
    )(params, cameras, asked)
    rows = lax.all_to_all(answers, AXES, 0, 0, tiled=True)
    row_grads = pl.pallas_call(
        lambda *refs: tile_kernel(owned, *refs),
        out_shape=full((LANES, 3 * LANES)),
        scratch_shapes=[
            pltpu.VMEM((3 * LANES, LANES), f32),
            pltpu.VMEM((24 * chunks, LANES), f32),
            pltpu.VMEM((9 * chunks, LANES), f32),
            pltpu.VMEM((entry_count, TILE_SIDE * TILE_SIDE), f32),
            pltpu.VMEM((entry_count, TILE_SIDE * TILE_SIDE), f32),
            pltpu.VMEM((16 * chunks, LANES), f32),
            pltpu.VMEM((FEATURES * chunks, LANES), f32),
        ],
        compiler_params=limits,
        name="tiles",
    )(entries, rank, rows, target[0])
    shares = lax.all_to_all(row_grads, AXES, 0, 0, tiled=True)
    return pl.pallas_call(
        lambda *refs: update_kernel(frame, *refs),
        out_shape=(full(params.shape),) * 3,
        scratch_shapes=[
            pltpu.VMEM((4 * LANES, LANES), f32),
            pltpu.VMEM((VIEWS * 16 * (owned // LANES), LANES), f32),
            pltpu.VMEM((64, owned), f32),
        ],
        compiler_params=limits,
        name="update",
    )(params, first_moment, second_moment, cameras, asked, shares, jnp.asarray(learning))


def solution(mesh):
    placed = (
        P(None, AXES),
        P(None, AXES),
        P(None, AXES),
        P(),
        P("views", "tiles", None, None),
        P("views", "tiles", None),
        P("views", "tiles"),
    )
    return jax.shard_map(
        per_device,
        mesh=mesh,
        in_specs=placed,
        out_specs=(P(None, AXES),) * 3,
        check_vma=False,
    )
```

```python
import jax
import jax.numpy as jnp
import numpy as np
from jax import lax
from jax.experimental import pallas as pl
from jax.experimental.pallas import tpu as pltpu
from jax.sharding import PartitionSpec as P

TILE_SIDE = 16
TILE_COLS = 32
ADAM_STEP = 1000
GROUP = 8
LANES = 128
VIEWS = 4
SLOTS = 32
HALF = SLOTS // 2
FEATURES = 9
AXES = ("views", "tiles")

f32 = jnp.float32
bf16 = jnp.bfloat16
i32 = jnp.int32

sh_zero = 0.28209479177387814
sh_first = 0.4886025119029199
sh_second = (
    1.0925484305920792,
    -1.0925484305920792,
    0.31539156525252005,
    -1.0925484305920792,
    0.5462742152960396,
)
sh_third = (
    -0.5900435899266435,
    2.890611442640554,
    -0.4570457994644658,
    0.3731763325901154,
    -0.4570457994644658,
    1.445305721320277,
    -0.5900435899266435,
)
beta_one = 0.9
beta_two = 0.999
adam_eps = 1e-15
log2_e = 1.4426950408889634


def matmul_three(left, right):
    return [
        [
            left[row_at][0] * right[0][col_at]
            + left[row_at][1] * right[1][col_at]
            + left[row_at][2] * right[2][col_at]
            for col_at in range(3)
        ]
        for row_at in range(3)
    ]


def rotation_entries(cos, sin):
    cos_a, cos_b, cos_c = cos
    sin_a, sin_b, sin_c = sin
    return [
        [cos_c * cos_b, cos_c * sin_b * sin_a - sin_c * cos_a, cos_c * sin_b * cos_a + sin_c * sin_a],
        [sin_c * cos_b, sin_c * sin_b * sin_a + cos_c * cos_a, sin_c * sin_b * cos_a - cos_c * sin_a],
        [-sin_b, cos_b * sin_a, cos_b * cos_a],
    ]


def sh_basis(along_x, along_y, along_z):
    square_x, square_y, square_z = (along_x * along_x, along_y * along_y, along_z * along_z)
    both_xy, both_yz, both_xz = (along_x * along_y, along_y * along_z, along_x * along_z)
    return [
        sh_zero + 0.0 * along_x,
        -sh_first * along_y,
        sh_first * along_z,
        -sh_first * along_x,
        sh_second[0] * both_xy,
        sh_second[1] * both_yz,
        sh_second[2] * (2.0 * square_z - square_x - square_y),
        sh_second[3] * both_xz,
        sh_second[4] * (square_x - square_y),
        sh_third[0] * along_y * (3.0 * square_x - square_y),
        sh_third[1] * both_xy * along_z,
        sh_third[2] * along_y * (4.0 * square_z - square_x - square_y),
        sh_third[3] * along_z * (2.0 * square_z - 3.0 * square_x - 3.0 * square_y),
        sh_third[4] * along_x * (4.0 * square_z - square_x - square_y),
        sh_third[5] * along_z * (square_x - square_y),
        sh_third[6] * along_x * (square_x - 3.0 * square_y),
    ]


def project(params, rotation, shift, focal_len, center_x, center_y):
    means = params[:3]
    point = [
        rotation[axis_at][0] * means[0]
        + rotation[axis_at][1] * means[1]
        + rotation[axis_at][2] * means[2]
        + shift[axis_at]
        for axis_at in range(3)
    ]
    inverse_z = 1.0 / point[2]
    screen_u = focal_len * point[0] * inverse_z + center_x
    screen_v = focal_len * point[1] * inverse_z + center_y
    scales = [jnp.exp(params[3 + axis_at]) for axis_at in range(3)]
    quat = params[6:10]
    inverse_norm = lax.rsqrt(
        quat[0] * quat[0] + quat[1] * quat[1] + quat[2] * quat[2] + quat[3] * quat[3]
    )
    real_part, imag_x, imag_y, imag_z = [part * inverse_norm for part in quat]
    spin = [
        [
            1.0 - 2.0 * (imag_y * imag_y + imag_z * imag_z),
            2.0 * (imag_x * imag_y - real_part * imag_z),
            2.0 * (imag_x * imag_z + real_part * imag_y),
        ],
        [
            2.0 * (imag_x * imag_y + real_part * imag_z),
            1.0 - 2.0 * (imag_x * imag_x + imag_z * imag_z),
            2.0 * (imag_y * imag_z - real_part * imag_x),
        ],
        [
            2.0 * (imag_x * imag_z - real_part * imag_y),
            2.0 * (imag_y * imag_z + real_part * imag_x),
            1.0 - 2.0 * (imag_x * imag_x + imag_y * imag_y),
        ],
    ]
    turned = matmul_three(rotation, spin)
    shaped = [
        [turned[row_at][col_at] * scales[col_at] for col_at in range(3)] for row_at in range(3)
    ]
    near_x = [
        focal_len * inverse_z * shaped[0][col_at]
        - focal_len * point[0] * inverse_z * inverse_z * shaped[2][col_at]
        for col_at in range(3)
    ]
    near_y = [
        focal_len * inverse_z * shaped[1][col_at]
        - focal_len * point[1] * inverse_z * inverse_z * shaped[2][col_at]
        for col_at in range(3)
    ]
    cov_a = near_x[0] * near_x[0] + near_x[1] * near_x[1] + near_x[2] * near_x[2] + 0.3
    cov_b = near_x[0] * near_y[0] + near_x[1] * near_y[1] + near_x[2] * near_y[2]
    cov_c = near_y[0] * near_y[0] + near_y[1] * near_y[1] + near_y[2] * near_y[2] + 0.3
    determinant = cov_a * cov_c - cov_b * cov_b
    offset = [
        means[axis_at]
        + rotation[0][axis_at] * shift[0]
        + rotation[1][axis_at] * shift[1]
        + rotation[2][axis_at] * shift[2]
        for axis_at in range(3)
    ]
    inverse_len = lax.rsqrt(offset[0] * offset[0] + offset[1] * offset[1] + offset[2] * offset[2])
    basis = sh_basis(offset[0] * inverse_len, offset[1] * inverse_len, offset[2] * inverse_len)
    colors = [
        0.5 + sum((basis[coef_at] * params[11 + 3 * coef_at + channel] for coef_at in range(16)))
        for channel in range(3)
    ]
    log_opacity = params[10] - jnp.log1p(jnp.exp(params[10]))
    return [
        screen_u,
        screen_v,
        cov_c / determinant,
        -cov_b / determinant,
        cov_a / determinant,
        log_opacity,
        colors[0],
        colors[1],
        colors[2],
    ]


def camera_terms(cameras_ref, owned):
    cameras = cameras_ref[...]
    cos, sin = jnp.cos(cameras), jnp.sin(cameras)

    def column(values, at):
        return jnp.broadcast_to(values[:, at : at + 1], (VIEWS, owned))

    rotation = rotation_entries(
        [column(cos, at) for at in range(3)], [column(sin, at) for at in range(3)]
    )
    return rotation, [column(cameras, 3 + at) for at in range(3)]


def iota(shape, dim):
    return lax.broadcasted_iota(i32, shape, dim)


def dot(left, right, left_dim, right_dim):
    return lax.dot_general(
        left, right, (((left_dim,), (right_dim,)), ((), ())), preferred_element_type=f32
    )


def pieces(values, count):
    out = []
    for at in range(count):
        part = values.astype(bf16)
        out.append(part)
        if at + 1 < count:
            values = values - part.astype(f32)
    return out


def rank_kernel(owned, entries_ref, rank_ref, request_ref):
    chunks = entries_ref.shape[0]
    entries = entries_ref[...]
    owner = lax.rem(lax.div(entries, owned), LANES)
    column = lax.rem(entries, owned)
    low = lax.rem(column, 256).astype(f32)
    high = lax.div(column, 256).astype(f32)
    before = jnp.where(iota((LANES, LANES), 0) < iota((LANES, LANES), 1), 1.0, 0.0)
    adder = jnp.concatenate([before, jnp.ones((LANES, LANES), f32)], axis=1).astype(bf16)
    owner_id = iota((LANES, LANES), 0)
    slot_id = iota((SLOTS, LANES), 0)
    base = jnp.zeros((LANES, LANES), f32)
    requests = jnp.zeros((LANES, 2 * SLOTS), f32)
    for at in range(chunks):
        hot = owner_id == owner[at : at + 1, :]
        hot_one = jnp.where(hot, 1.0, 0.0).astype(bf16)
        counts = dot(hot_one, adder, 1, 0)
        rank = jnp.sum(
            jnp.where(hot, counts[:, :LANES] + base, 0.0), axis=0, keepdims=True
        ).astype(i32)
        base = base + counts[:, LANES:]
        rank_ref[at : at + 1, :] = rank
        slot = slot_id == rank
        wanted = jnp.concatenate(
            [
                jnp.where(slot, low[at : at + 1, :], 0.0),
                jnp.where(slot, high[at : at + 1, :], 0.0),
            ],
            axis=0,
        ).astype(bf16)
        requests = requests + dot(hot_one, wanted, 1, 1)
    request_ref[...] = requests[:, :SLOTS] + 256.0 * requests[:, SLOTS:]


def flipped_requests(asked_ref):
    asked = asked_ref[...]
    wide = jnp.concatenate([asked, jnp.zeros((LANES, LANES - SLOTS), f32)], axis=1)
    return wide.T[:SLOTS, :].astype(i32)


def answer_kernel(frame, params_ref, cameras_ref, asked_ref, rows_ref):
    owned = params_ref.shape[1]
    rotation, shift = camera_terms(cameras_ref, owned)
    params = [jnp.broadcast_to(params_ref[at : at + 1, :], (VIEWS, owned)) for at in range(59)]
    projected = project(params, rotation, shift, *frame)
    asked = flipped_requests(asked_ref)
    chunk_of = lax.div(asked, LANES)
    lane_of = lax.rem(asked, LANES)
    view_of = lax.div(iota((SLOTS, LANES), 1), LANES // VIEWS)
    chosen = [jnp.zeros((SLOTS, LANES), f32) for _ in range(FEATURES)]
    for view in range(VIEWS):
        for chunk in range(owned // LANES):
            mask = (view_of == view) & (chunk_of == chunk)
            for at in range(FEATURES):
                source = jnp.broadcast_to(
                    projected[at][view : view + 1, chunk * LANES : (chunk + 1) * LANES],
                    (SLOTS, LANES),
                )
                found = jnp.take_along_axis(source, lane_of, axis=1, mode="promise_in_bounds")
                chosen[at] = jnp.where(mask, found, chosen[at])
    stack = [
        chosen[at][half * HALF : (half + 1) * HALF] for half in range(2) for at in range(FEATURES)
    ]
    stack.append(jnp.zeros((3 * LANES - SLOTS * FEATURES, LANES), f32))
    stack = jnp.concatenate(stack, axis=0)
    for part in range(3):
        rows_ref[:, part * LANES : (part + 1) * LANES] = stack[
            part * LANES : (part + 1) * LANES
        ].T


def slot_columns(entries, rank, owned):
    owner = lax.rem(lax.div(entries, owned), LANES)
    return lax.div(rank, HALF) * LANES + owner, lax.rem(rank, HALF)


def tile_kernel(
    owned,
    entries_ref,
    rank_ref,
    rows_ref,
    target_ref,
    grads_ref,
    hot_ref,
    picked_ref,
    coef_ref,
    color_ref,
    alpha_ref,
    weight_ref,
    high_ref,
    middle_ref,
    low_ref,
    pull_ref,
    moment_ref,
    grad_ref,
    spread_ref,
):
    chunks = entries_ref.shape[0]
    groups = 2
    per_group = chunks // groups
    pixels = TILE_SIDE * TILE_SIDE
    steps = LANES // GROUP
    span = FEATURES * HALF
    first_tile = lax.axis_index("tiles") * (groups * GROUP)

    entries = entries_ref[...]
    live = entries < owned * LANES
    place, below = slot_columns(entries, rank_ref[...], owned)
    place = place.astype(f32)
    place_id = iota((2 * LANES, LANES), 0).astype(f32).astype(bf16)
    for at in range(chunks):
        row = jnp.broadcast_to(place[at : at + 1, :], (2 * LANES, LANES)).astype(bf16)
        hot_ref[:, at * LANES : (at + 1) * LANES] = jnp.where(
            place_id == row, jnp.ones((), bf16), jnp.zeros((), bf16)
        )

    flipped = jnp.concatenate(
        [rows_ref[:, part * LANES : (part + 1) * LANES].T for part in range(3)], axis=0
    )
    table = jnp.concatenate([flipped[:span], flipped[span : 2 * span]], axis=1)
    table = jnp.concatenate(pieces(table, 3), axis=0)
    half_id = iota((HALF, LANES), 0)
    for at in range(0, chunks, 2):
        found = dot(table, hot_ref[:, at * LANES : (at + 2) * LANES], 1, 0)
        found = found[:span] + (found[span : 2 * span] + found[2 * span :])
        for side in range(2):
            mask = half_id == below[at + side : at + side + 1, :]
            for feature in range(FEATURES):
                values = found[
                    feature * HALF : (feature + 1) * HALF, side * LANES : (side + 1) * LANES
                ]
                row = feature * chunks + at + side
                picked_ref[row : row + 1, :] = jnp.sum(
                    jnp.where(mask, values, 0.0), axis=0, keepdims=True
                )
    shape = (chunks, LANES)
    chosen = [picked_ref[at * chunks : (at + 1) * chunks, :] for at in range(FEATURES)]

    tile = first_tile + lax.div(iota(shape, 0), per_group) * GROUP + lax.rem(iota(shape, 1), GROUP)
    middle_x = (lax.rem(tile, TILE_COLS) * TILE_SIDE + TILE_SIDE // 2).astype(f32)
    middle_y = (lax.div(tile, TILE_COLS) * TILE_SIDE + TILE_SIDE // 2).astype(f32)
    at_u = chosen[0] - middle_x
    at_v = chosen[1] - middle_y
    conic_a, conic_b, conic_c = chosen[2], chosen[3], chosen[4]
    by_u = conic_a * at_u + conic_b * at_v
    by_v = conic_b * at_u + conic_c * at_v
    coefs = [
        jnp.where(live, log2_e * (chosen[5] - 0.5 * (at_u * by_u + at_v * by_v)), -1e4),
        jnp.where(live, log2_e * by_u, 0.0),
        jnp.where(live, log2_e * by_v, 0.0),
        jnp.where(live, (-0.5 * log2_e) * conic_a, 0.0),
        jnp.where(live, -log2_e * conic_b, 0.0),
        jnp.where(live, (-0.5 * log2_e) * conic_c, 0.0),
    ]
    for at in range(8):
        split = pieces(coefs[at], 3) if at < 6 else [jnp.zeros(shape, bf16)] * 3
        for part in range(3):
            row = (part * 8 + at) * chunks
            coef_ref[row : row + chunks, :] = split[part].astype(f32)
    for at in range(3):
        split = pieces(chosen[6 + at], 3)
        for part in range(3):
            row = (part * 3 + at) * chunks
            color_ref[row : row + chunks, :] = split[part].astype(f32)

    pixel = iota((8, pixels), 1)
    row8 = iota((8, pixels), 0)
    off_x = lax.rem(pixel, TILE_SIDE).astype(f32) - 7.5
    off_y = lax.div(pixel, TILE_SIDE).astype(f32) - 7.5
    base = jnp.where(row8 == 0, 1.0, 0.0)
    for at, values in enumerate([off_x, off_y, off_x * off_x, off_x * off_y, off_y * off_y]):
        base = jnp.where(row8 == at + 1, values, base)
    base_two = jnp.concatenate([base, base], axis=1).astype(bf16)
    base_three = jnp.concatenate([base, base, base], axis=0).astype(bf16)
    same_tile = lax.rem(iota((GROUP, LANES), 1), GROUP) == iota((GROUP, LANES), 0)

    def rows_of(chunk):
        return pl.ds(pl.multiple_of(chunk * LANES, LANES), LANES)

    def color_rows(chunk):
        rows = []
        for part in range(9):
            row = color_ref[pl.ds(part * chunks + chunk, 1), :]
            rows.append(jnp.where(same_tile, jnp.broadcast_to(row, (GROUP, LANES)), 0.0))
        return jnp.concatenate(rows, axis=0).astype(bf16)

    def shade(at):
        for group in range(groups):
            chunk = group * per_group + at
            coef = coef_ref[pl.ds(chunk, 24, stride=chunks), :].astype(bf16)
            alpha_ref[rows_of(chunk), :] = jnp.exp2(dot(coef, base_three, 0, 0))

    def weigh(at, clears):
        out = []
        for group in range(groups):
            clear = clears[group]
            rows = rows_of(group * per_group + at)
            alpha = alpha_ref[rows, :]
            weights = []
            for step in range(steps):
                weight = alpha[step * GROUP : (step + 1) * GROUP, :] * clear
                clear = clear - weight
                weights.append(weight)
            weight = jnp.concatenate(weights, axis=0)
            weight_ref[rows, :] = weight
            high_ref[rows, :], middle_ref[rows, :], low_ref[rows, :] = pieces(weight, 3)
            out.append(clear)
        return tuple(out)

    def blend(at, renders):
        out = []
        for group in range(groups):
            chunk = group * per_group + at
            rows = rows_of(chunk)
            colors = color_rows(chunk)
            colors = jnp.concatenate([colors, colors, colors], axis=1)
            parts = jnp.concatenate(
                [high_ref[rows, :], middle_ref[rows, :], low_ref[rows, :]], axis=0
            )
            out.append(renders[group] + dot(colors, parts, 1, 0))
        return tuple(out)

    clears = (jnp.ones((GROUP, pixels), f32),) * groups
    renders = (jnp.zeros((72, pixels), f32),) * groups
    shade(0)
    shade(1)
    clears = weigh(0, clears)

    def forward(at, carry):
        clears, renders = carry
        shade(at + 1)
        renders = blend(at - 1, renders)
        clears = weigh(at, clears)
        return clears, renders

    clears, renders = lax.fori_loop(1, per_group - 1, forward, (clears, renders))
    renders = blend(per_group - 2, renders)
    clears = weigh(per_group - 1, clears)
    renders = blend(per_group - 1, renders)

    signs, sign_twos, sign_threes = [], [], []
    for group in range(groups):
        render = renders[group]
        render = render[:24] + (render[24:48] + render[48:])
        rows = []
        for at in range(3):
            gap = (
                render[at * GROUP : (at + 1) * GROUP, :]
                - target_ref[group * GROUP : (group + 1) * GROUP, at, :]
            )
            rows.append(jnp.where(gap > 0.0, 1.0, jnp.where(gap < 0.0, -1.0, 0.0)))
        sign = jnp.concatenate(rows, axis=0)
        sign_twos.append(jnp.concatenate([sign, sign], axis=1).astype(bf16))
        sign_threes.append(jnp.concatenate([sign, sign, sign], axis=0).astype(bf16))

    def draw(at):
        for group in range(groups):
            chunk = group * per_group + at
            pull_ref[rows_of(chunk), :] = dot(color_rows(chunk), sign_threes[group], 0, 0)

    def unweigh(at, behinds):
        out = []
        for group in range(groups):
            behind = behinds[group]
            rows = rows_of(group * per_group + at)
            pull, alpha, weight = pull_ref[rows, :], alpha_ref[rows, :], weight_ref[rows, :]
            by_alpha = [None] * steps
            for step in reversed(range(steps)):
                part = slice(step * GROUP, (step + 1) * GROUP)
                gap = pull[part, :] - behind
                by_alpha[step] = weight[part, :] * gap
                behind = behind + alpha[part, :] * gap
            low_ref[rows, :], spread_ref[rows, :] = pieces(jnp.concatenate(by_alpha, axis=0), 2)
            out.append(behind)
        return tuple(out)

    def total(at):
        for group in range(groups):
            chunk = group * per_group + at
            rows = rows_of(chunk)
            row = pl.multiple_of(chunk * 16, 16)
            parts = jnp.concatenate([low_ref[rows, :], spread_ref[rows, :]], axis=1)
            moment_ref[pl.ds(row, 8), :] = dot(base_two, parts, 1, 1)
            parts = jnp.concatenate([high_ref[rows, :], middle_ref[rows, :]], axis=1)
            by_color = dot(sign_twos[group], parts, 1, 1)
            for channel in range(3):
                moment_ref[pl.ds(row + 8 + channel, 1), :] = jnp.sum(
                    jnp.where(same_tile, by_color[channel * GROUP : (channel + 1) * GROUP], 0.0),
                    axis=0,
                    keepdims=True,
                )

    behinds = (jnp.zeros((GROUP, pixels), f32),) * groups
    draw(per_group - 1)
    draw(per_group - 2)
    behinds = unweigh(per_group - 1, behinds)

    def backward(back, behinds):
        at = per_group - 1 - back
        draw(at - 1)
        total(at + 1)
        return unweigh(at, behinds)

    behinds = lax.fori_loop(1, per_group - 1, backward, behinds)
    total(1)
    behinds = unweigh(0, behinds)
    total(0)

    sums = [moment_ref[pl.ds(at, chunks, stride=16), :] for at in range(6)]
    sum_x = sums[1] - at_u * sums[0]
    sum_y = sums[2] - at_v * sums[0]
    sum_xx = sums[3] - 2.0 * at_u * sums[1] + at_u * at_u * sums[0]
    sum_xy = sums[4] - at_u * sums[2] - at_v * sum_x
    sum_yy = sums[5] - 2.0 * at_v * sums[2] + at_v * at_v * sums[0]
    grads = [
        conic_a * sum_x + conic_b * sum_y,
        conic_b * sum_x + conic_c * sum_y,
        -0.5 * sum_xx,
        -sum_xy,
        -0.5 * sum_yy,
        sums[0],
    ] + [moment_ref[pl.ds(8 + at, chunks, stride=16), :] for at in range(3)]

    half_one = half_id.astype(f32).astype(bf16)
    below = below.astype(f32)
    grads = [pieces(jnp.where(live, grad, 0.0), 2) for grad in grads]
    grads = [[part.astype(f32) for part in split] for split in grads]
    for at in range(chunks):
        mask = half_one == jnp.broadcast_to(below[at : at + 1, :], (HALF, LANES)).astype(bf16)
        for part in range(2):
            for feature in range(FEATURES):
                row = grads[feature][part][at : at + 1, :]
                grad_ref[
                    part * span + feature * HALF : part * span + (feature + 1) * HALF,
                    at * LANES : (at + 1) * LANES,
                ] = jnp.where(
                    mask,
                    jnp.broadcast_to(row, (HALF, LANES)).astype(bf16),
                    jnp.zeros((), bf16),
                )
    sent = dot(grad_ref[...], hot_ref[...], 1, 1)
    sent = sent[:span] + sent[span:]
    sent = jnp.concatenate(
        [sent[:, :LANES], sent[:, LANES:], jnp.zeros((3 * LANES - 2 * span, LANES), f32)], axis=0
    )
    for part in range(3):
        grads_ref[:, part * LANES : (part + 1) * LANES] = sent[
            part * LANES : (part + 1) * LANES, :
        ].T


def tiles_call(entries, rank, rows, target, owned):
    chunks = entries.shape[0]
    pixels = TILE_SIDE * TILE_SIDE
    count = chunks * LANES

    def plane(dtype):
        return pltpu.VMEM((count, pixels), dtype)

    return pl.pallas_call(
        lambda *refs: tile_kernel(owned, *refs),
        out_shape=jax.ShapeDtypeStruct((LANES, 3 * LANES), f32),
        scratch_shapes=[
            pltpu.VMEM((2 * LANES, count), bf16),
            pltpu.VMEM((FEATURES * chunks, LANES), f32),
            pltpu.VMEM((24 * chunks, LANES), f32),
            pltpu.VMEM((9 * chunks, LANES), f32),
            plane(f32),
            plane(f32),
            plane(bf16),
            plane(bf16),
            plane(bf16),
            plane(f32),
            pltpu.VMEM((16 * chunks, LANES), f32),
            pltpu.VMEM((2 * FEATURES * HALF, count), bf16),
            plane(bf16),
        ],
        compiler_params=pltpu.CompilerParams(vmem_limit_bytes=48 * 1024 * 1024),
        name="tiles",
    )(entries, rank, rows, target)


def update_kernel(
    frame,
    params_ref,
    first_ref,
    second_ref,
    cameras_ref,
    asked_ref,
    grads_ref,
    rates_ref,
    new_params_ref,
    new_first_ref,
    new_second_ref,
    source_ref,
    dense_ref,
    gradient_ref,
):
    owned = params_ref.shape[1]
    asked = flipped_requests(asked_ref)
    for part in range(3):
        source_ref[part * LANES : (part + 1) * LANES, :] = grads_ref[
            :, part * LANES : (part + 1) * LANES
        ].T
    source_ref[3 * LANES :, :] = jnp.zeros((LANES, LANES), f32)
    view_of = lax.div(iota((16, LANES), 1), LANES // VIEWS)
    column_id = iota((owned, LANES), 0)
    dense = jnp.zeros((2 * VIEWS * 16, owned), f32)
    for slot in range(SLOTS):
        hot = jnp.where(column_id == asked[slot : slot + 1, :], 1.0, 0.0).astype(bf16)
        first = slot // HALF * FEATURES * HALF + slot % HALF
        values = source_ref[pl.ds(first, 16, stride=HALF), :]
        values = jnp.concatenate(
            [jnp.where(view_of == view, values, 0.0) for view in range(VIEWS)], axis=0
        )
        high, low = pieces(values, 2)
        dense = dense + dot(jnp.concatenate([high, low], axis=0), hot, 1, 1)
    dense = dense[: VIEWS * 16] + dense[VIEWS * 16 :]
    spans = range(owned // LANES)
    for span in spans:
        dense_ref[span * VIEWS * 16 : (span + 1) * VIEWS * 16, :] = dense[
            :, span * LANES : (span + 1) * LANES
        ]
    cotangents = [
        jnp.concatenate(
            [dense_ref[pl.ds(span * VIEWS * 16 + at, VIEWS, stride=16), :] for span in spans], axis=1
        )
        for at in range(FEATURES)
    ]

    rotation, shift = camera_terms(cameras_ref, owned)
    params = [jnp.broadcast_to(params_ref[at : at + 1, :], (VIEWS, owned)) for at in range(59)]
    _, pullback = jax.vjp(lambda values: project(values, rotation, shift, *frame), params)
    by_params = pullback(cotangents)[0]
    for at in range(59):
        gradient_ref[at : at + 1, :] = jnp.sum(by_params[at], axis=0, keepdims=True)
    gradient = gradient_ref[:59, :]
    new_first = beta_one * first_ref[...] + (1.0 - beta_one) * gradient
    new_second = beta_two * second_ref[...] + (1.0 - beta_two) * gradient * gradient
    new_first_ref[...] = new_first
    new_second_ref[...] = new_second
    step_size = rates_ref[...] * (new_first / (1.0 - beta_one**ADAM_STEP))
    new_params_ref[...] = params_ref[...] - step_size / (
        jnp.sqrt(new_second / (1.0 - beta_two**ADAM_STEP)) + adam_eps
    )


learning = np.concatenate(
    [
        np.full(3, 0.00016),
        np.full(3, 0.005),
        np.full(4, 0.001),
        np.full(1, 0.05),
        np.full(3, 0.0025),
        np.full(45, 0.000125),
    ]
).astype(np.float32)[:, None]


def per_device(params, first_moment, second_moment, cameras, target, lists, lengths):
    owned = params.shape[1]
    list_size = lists.shape[2]
    tile_dev = lists.shape[1]
    entry_count = tile_dev * list_size
    chunks = entry_count // LANES
    width = TILE_COLS * TILE_SIDE
    height = tile_dev * lax.axis_size("tiles") // TILE_COLS * TILE_SIDE
    frame = (float(width), 0.5 * width, 0.5 * height)
    limits = pltpu.CompilerParams(vmem_limit_bytes=48 * 1024 * 1024)

    dead = jnp.arange(list_size, dtype=i32)[None, :] >= lengths[0][:, None]
    entries = lists[0] + jnp.where(dead, owned * LANES, 0)
    entries = (
        entries.reshape(tile_dev // GROUP, GROUP, list_size).transpose(0, 2, 1).reshape(chunks, LANES)
    )

    def full(shape, dtype=f32):
        return jax.ShapeDtypeStruct(shape, dtype)

    rank, requests = pl.pallas_call(
        lambda *refs: rank_kernel(owned, *refs),
        out_shape=(full((chunks, LANES), i32), full((LANES, SLOTS))),
        compiler_params=limits,
        name="rank",
    )(entries)
    asked = lax.all_to_all(requests, AXES, 0, 0, tiled=True)
    answers = pl.pallas_call(
        lambda *refs: answer_kernel(frame, *refs),
        out_shape=full((LANES, 3 * LANES)),
        compiler_params=limits,
        name="answer",
    )(params, cameras, asked)
    rows = lax.all_to_all(answers, AXES, 0, 0, tiled=True)
    row_grads = tiles_call(entries, rank, rows, target[0], owned)
    shares = lax.all_to_all(row_grads, AXES, 0, 0, tiled=True)
    return pl.pallas_call(
        lambda *refs: update_kernel(frame, *refs),
        out_shape=(full(params.shape),) * 3,
        scratch_shapes=[
            pltpu.VMEM((4 * LANES, LANES), f32),
            pltpu.VMEM((VIEWS * 16 * (owned // LANES), LANES), f32),
            pltpu.VMEM((64, owned), f32),
        ],
        compiler_params=limits,
        name="update",
    )(params, first_moment, second_moment, cameras, asked, shares, jnp.asarray(learning))


def solution(mesh):
    placed = (
        P(None, AXES),
        P(None, AXES),
        P(None, AXES),
        P(),
        P("views", "tiles", None, None),
        P("views", "tiles", None),
        P("views", "tiles"),
    )
    return jax.shard_map(
        per_device,
        mesh=mesh,
        in_specs=placed,
        out_specs=(P(None, AXES),) * 3,
        check_vma=False,
    )
```

```python
import jax
import jax.numpy as jnp
from jax import lax
from jax.experimental import pallas as pl
from jax.experimental.pallas import tpu as pltpu
from jax.sharding import PartitionSpec as P

TILE_SIDE = 16
TILE_COLS = 32
ADAM_STEP = 1000
GROUP = 8
LANES = 128
VIEWS = 4
SLOTS = 32
HALF = SLOTS // 2
BLOCK = 8
FEATURES = 9
AXES = ("views", "tiles")

f32 = jnp.float32
bf16 = jnp.bfloat16
i32 = jnp.int32

sh_zero = 0.28209479177387814
sh_first = 0.4886025119029199
sh_second = (
    1.0925484305920792,
    -1.0925484305920792,
    0.31539156525252005,
    -1.0925484305920792,
    0.5462742152960396,
)
sh_third = (
    -0.5900435899266435,
    2.890611442640554,
    -0.4570457994644658,
    0.3731763325901154,
    -0.4570457994644658,
    1.445305721320277,
    -0.5900435899266435,
)
beta_one = 0.9
beta_two = 0.999
adam_eps = 1e-15
log2_e = 1.4426950408889634


def matmul_three(left, right):
    return [
        [
            left[row_at][0] * right[0][col_at]
            + left[row_at][1] * right[1][col_at]
            + left[row_at][2] * right[2][col_at]
            for col_at in range(3)
        ]
        for row_at in range(3)
    ]


def rotation_entries(cos, sin):
    cos_a, cos_b, cos_c = cos
    sin_a, sin_b, sin_c = sin
    return [
        [cos_c * cos_b, cos_c * sin_b * sin_a - sin_c * cos_a, cos_c * sin_b * cos_a + sin_c * sin_a],
        [sin_c * cos_b, sin_c * sin_b * sin_a + cos_c * cos_a, sin_c * sin_b * cos_a - cos_c * sin_a],
        [-sin_b, cos_b * sin_a, cos_b * cos_a],
    ]


def sh_basis(along_x, along_y, along_z):
    square_x, square_y, square_z = (along_x * along_x, along_y * along_y, along_z * along_z)
    both_xy, both_yz, both_xz = (along_x * along_y, along_y * along_z, along_x * along_z)
    return [
        sh_zero + 0.0 * along_x,
        -sh_first * along_y,
        sh_first * along_z,
        -sh_first * along_x,
        sh_second[0] * both_xy,
        sh_second[1] * both_yz,
        sh_second[2] * (2.0 * square_z - square_x - square_y),
        sh_second[3] * both_xz,
        sh_second[4] * (square_x - square_y),
        sh_third[0] * along_y * (3.0 * square_x - square_y),
        sh_third[1] * both_xy * along_z,
        sh_third[2] * along_y * (4.0 * square_z - square_x - square_y),
        sh_third[3] * along_z * (2.0 * square_z - 3.0 * square_x - 3.0 * square_y),
        sh_third[4] * along_x * (4.0 * square_z - square_x - square_y),
        sh_third[5] * along_z * (square_x - square_y),
        sh_third[6] * along_x * (square_x - 3.0 * square_y),
    ]


def project(params, rotation, shift, focal_len, center_x, center_y):
    means = params[:3]
    point = [
        rotation[axis_at][0] * means[0]
        + rotation[axis_at][1] * means[1]
        + rotation[axis_at][2] * means[2]
        + shift[axis_at]
        for axis_at in range(3)
    ]
    inverse_z = 1.0 / point[2]
    screen_u = focal_len * point[0] * inverse_z + center_x
    screen_v = focal_len * point[1] * inverse_z + center_y
    scales = [jnp.exp(params[3 + axis_at]) for axis_at in range(3)]
    quat = params[6:10]
    inverse_norm = lax.rsqrt(
        quat[0] * quat[0] + quat[1] * quat[1] + quat[2] * quat[2] + quat[3] * quat[3]
    )
    real_part, imag_x, imag_y, imag_z = [part * inverse_norm for part in quat]
    spin = [
        [
            1.0 - 2.0 * (imag_y * imag_y + imag_z * imag_z),
            2.0 * (imag_x * imag_y - real_part * imag_z),
            2.0 * (imag_x * imag_z + real_part * imag_y),
        ],
        [
            2.0 * (imag_x * imag_y + real_part * imag_z),
            1.0 - 2.0 * (imag_x * imag_x + imag_z * imag_z),
            2.0 * (imag_y * imag_z - real_part * imag_x),
        ],
        [
            2.0 * (imag_x * imag_z - real_part * imag_y),
            2.0 * (imag_y * imag_z + real_part * imag_x),
            1.0 - 2.0 * (imag_x * imag_x + imag_y * imag_y),
        ],
    ]
    turned = matmul_three(rotation, spin)
    shaped = [
        [turned[row_at][col_at] * scales[col_at] for col_at in range(3)] for row_at in range(3)
    ]
    near_x = [
        focal_len * inverse_z * shaped[0][col_at]
        - focal_len * point[0] * inverse_z * inverse_z * shaped[2][col_at]
        for col_at in range(3)
    ]
    near_y = [
        focal_len * inverse_z * shaped[1][col_at]
        - focal_len * point[1] * inverse_z * inverse_z * shaped[2][col_at]
        for col_at in range(3)
    ]
    cov_a = near_x[0] * near_x[0] + near_x[1] * near_x[1] + near_x[2] * near_x[2] + 0.3
    cov_b = near_x[0] * near_y[0] + near_x[1] * near_y[1] + near_x[2] * near_y[2]
    cov_c = near_y[0] * near_y[0] + near_y[1] * near_y[1] + near_y[2] * near_y[2] + 0.3
    determinant = cov_a * cov_c - cov_b * cov_b
    offset = [
        means[axis_at]
        + rotation[0][axis_at] * shift[0]
        + rotation[1][axis_at] * shift[1]
        + rotation[2][axis_at] * shift[2]
        for axis_at in range(3)
    ]
    inverse_len = lax.rsqrt(offset[0] * offset[0] + offset[1] * offset[1] + offset[2] * offset[2])
    basis = sh_basis(offset[0] * inverse_len, offset[1] * inverse_len, offset[2] * inverse_len)
    colors = [
        0.5 + sum((basis[coef_at] * params[11 + 3 * coef_at + channel] for coef_at in range(16)))
        for channel in range(3)
    ]
    log_opacity = params[10] - jnp.log1p(jnp.exp(params[10]))
    return [
        screen_u,
        screen_v,
        cov_c / determinant,
        -cov_b / determinant,
        cov_a / determinant,
        log_opacity,
        colors[0],
        colors[1],
        colors[2],
    ]


def camera_terms(cameras_ref, owned):
    cameras = cameras_ref[...]
    cos, sin = jnp.cos(cameras), jnp.sin(cameras)

    def column(values, at):
        return jnp.broadcast_to(values[:, at : at + 1], (VIEWS, owned))

    rotation = rotation_entries(
        [column(cos, at) for at in range(3)], [column(sin, at) for at in range(3)]
    )
    return rotation, [column(cameras, 3 + at) for at in range(3)]


def iota(shape, dim):
    return lax.broadcasted_iota(i32, shape, dim)


def dot(left, right, left_dim, right_dim):
    return lax.dot_general(
        left, right, (((left_dim,), (right_dim,)), ((), ())), preferred_element_type=f32
    )


def pieces(values, count):
    out = []
    for at in range(count):
        part = values.astype(bf16)
        out.append(part)
        if at + 1 < count:
            values = values - part.astype(f32)
    return out


def one_hot(ids, row):
    row = jnp.broadcast_to(row, (16, row.shape[1])).astype(bf16)
    row = jnp.concatenate([row] * (ids.shape[0] // 16), axis=0)
    return jnp.where(ids == row, jnp.ones((), bf16), jnp.zeros((), bf16))


def small_ids(count):
    return iota((count, LANES), 0).astype(f32).astype(bf16)


def rank_kernel(
    owned, lists_ref, lengths_ref, entries_ref, rank_ref, request_ref, hot_ref, wanted_ref
):
    chunks = entries_ref.shape[0]
    per_group = chunks // 2
    steps = LANES // GROUP
    lengths = jnp.concatenate(
        [lengths_ref[...], jnp.zeros((1, LANES - lengths_ref.shape[1]), i32)], axis=1
    )
    lengths = jnp.broadcast_to(lengths, (GROUP, LANES))
    lane = iota((GROUP, LANES), 1)
    tile = lax.rem(lane, GROUP)
    spot = iota((GROUP, LANES), 0) * steps + lax.div(lane, GROUP)
    for group in range(2):
        length = jnp.take_along_axis(
            lengths, group * GROUP + tile, axis=1, mode="promise_in_bounds"
        )
        for half in range(per_group // GROUP):
            made = jnp.zeros((GROUP, LANES), i32)
            for at in range(GROUP):
                row = group * GROUP + at
                source = jnp.broadcast_to(
                    lists_ref[row : row + 1, half * LANES : (half + 1) * LANES], (GROUP, LANES)
                )
                found = jnp.take_along_axis(source, spot, axis=1, mode="promise_in_bounds")
                made = jnp.where(tile == at, found, made)
            dead = spot + half * LANES >= length
            row = group * per_group + half * GROUP
            entries_ref[row : row + GROUP, :] = jnp.where(dead, made + owned * LANES, made)
    entries = entries_ref[...]
    owner = lax.rem(lax.div(entries, owned), LANES)
    owner_row = owner.astype(f32)
    column = lax.rem(entries, owned)
    low = lax.rem(column, 256).astype(f32)
    high = lax.div(column, 256).astype(f32)
    before = jnp.where(iota((LANES, LANES), 0) < iota((LANES, LANES), 1), 1.0, 0.0)
    adder = jnp.concatenate([before, jnp.ones((LANES, LANES), f32)], axis=1).astype(bf16)
    owner_id = iota((LANES, LANES), 0)
    owner_one = small_ids(LANES)
    slot_one = small_ids(SLOTS)
    base = jnp.zeros((LANES, LANES), f32)
    for at in range(chunks):
        lanes = slice(at * LANES, (at + 1) * LANES)
        hot = one_hot(owner_one, owner_row[at : at + 1, :])
        hot_ref[:, lanes] = hot
        counts = dot(hot, adder, 1, 0)
        rank = jnp.sum(
            jnp.where(owner_id == owner[at : at + 1, :], counts[:, :LANES] + base, 0.0),
            axis=0,
            keepdims=True,
        )
        base = base + counts[:, LANES:]
        rank_ref[at : at + 1, :] = rank.astype(i32)
        slot = one_hot(slot_one, rank)
        wanted_ref[:, lanes] = jnp.concatenate(
            [
                slot * jnp.broadcast_to(part[at : at + 1, :], (SLOTS, LANES)).astype(bf16)
                for part in (low, high)
            ],
            axis=0,
        )
    requests = dot(hot_ref[...], wanted_ref[...], 1, 1)
    request_ref[...] = requests[:, :SLOTS] + 256.0 * requests[:, SLOTS:]


def flipped_requests(asked_ref):
    asked = asked_ref[...]
    wide = jnp.concatenate([asked, jnp.zeros((LANES, LANES - SLOTS), f32)], axis=1)
    return wide.T[:SLOTS, :].astype(i32)


def project_kernel(frame, params_ref, cameras_ref, table_ref):
    owned = params_ref.shape[1]
    rotation, shift = camera_terms(cameras_ref, owned)
    params = [jnp.broadcast_to(params_ref[at : at + 1, :], (VIEWS, owned)) for at in range(59)]
    for at, values in enumerate(project(params, rotation, shift, *frame)):
        table_ref[at * VIEWS : (at + 1) * VIEWS, :] = values


def spread_rows(stack, out_ref):
    for part in range(3):
        out_ref[pl.ds(part, LANES, stride=3), :] = stack[part * LANES : (part + 1) * LANES].T


def gathered_rows(rows_ref):
    return jnp.concatenate(
        [rows_ref[pl.ds(part, LANES, stride=3), :].T for part in range(3)], axis=0
    )


def answer_kernel(table_ref, asked_ref, rows_ref):
    owned = table_ref.shape[1]
    asked = flipped_requests(asked_ref)
    chunk_of = lax.div(asked, LANES)
    lane_of = lax.rem(asked, LANES)
    view_of = lax.div(iota((SLOTS, LANES), 1), LANES // VIEWS)
    chosen = [jnp.zeros((SLOTS, LANES), f32) for _ in range(FEATURES)]
    for view in range(VIEWS):
        for chunk in range(owned // LANES):
            mask = (view_of == view) & (chunk_of == chunk)
            for at in range(FEATURES):
                row = at * VIEWS + view
                source = jnp.broadcast_to(
                    table_ref[row : row + 1, chunk * LANES : (chunk + 1) * LANES], (SLOTS, LANES)
                )
                found = jnp.take_along_axis(source, lane_of, axis=1, mode="promise_in_bounds")
                chosen[at] = jnp.where(mask, found, chosen[at])
    stack = [
        chosen[at][half * HALF : (half + 1) * HALF] for half in range(2) for at in range(FEATURES)
    ]
    stack.append(jnp.zeros((3 * LANES - SLOTS * FEATURES, LANES), f32))
    spread_rows(jnp.concatenate(stack, axis=0), rows_ref)


def prepare_kernel(owned, entries_ref, rank_ref, asked_ref, hot_ref, column_ref):
    ids = small_ids(2 * LANES)
    place, _ = slot_columns(entries_ref[...], rank_ref[...], owned)
    place = place.astype(f32)
    for at in range(entries_ref.shape[0]):
        hot_ref[:, at * LANES : (at + 1) * LANES] = one_hot(ids, place[at : at + 1, :])
    low = lax.rem(flipped_requests(asked_ref), 2 * LANES).astype(f32)
    for at in range(SLOTS):
        column_ref[:, at * LANES : (at + 1) * LANES] = one_hot(ids, low[at : at + 1, :])


def slot_columns(entries, rank, owned):
    owner = lax.rem(lax.div(entries, owned), LANES)
    return lax.div(rank, HALF) * LANES + owner, lax.rem(rank, HALF)


def tile_kernel(
    owned,
    entries_ref,
    rank_ref,
    hot_ref,
    rows_ref,
    target_ref,
    grads_ref,
    picked_ref,
    coef_ref,
    color_ref,
    alpha_ref,
    weight_ref,
    high_ref,
    middle_ref,
    low_ref,
    pull_ref,
    moment_ref,
    grad_ref,
    spread_ref,
    paint_ref,
):
    chunks = entries_ref.shape[0]
    groups = 2
    per_group = chunks // groups
    pixels = TILE_SIDE * TILE_SIDE
    steps = LANES // GROUP
    span = FEATURES * HALF
    first_tile = lax.axis_index("tiles") * (groups * GROUP)

    entries = entries_ref[...]
    live = entries < owned * LANES
    _, below = slot_columns(entries, rank_ref[...], owned)

    flipped = gathered_rows(rows_ref)
    table = jnp.concatenate([flipped[:span], flipped[span : 2 * span]], axis=1)
    table = jnp.concatenate(pieces(table, 3), axis=0)
    for at in range(0, chunks, 2):
        found = dot(table, hot_ref[:, at * LANES : (at + 2) * LANES], 1, 0)
        found = found[:span] + (found[span : 2 * span] + found[2 * span :])
        for side in range(2):
            row = jnp.broadcast_to(below[at + side : at + side + 1, :], (8, LANES))
            index, upper = lax.rem(row, 8), row >= 8
            for feature in range(FEATURES):
                first, second = [
                    jnp.take_along_axis(
                        found[part : part + 8, side * LANES : (side + 1) * LANES],
                        index,
                        axis=0,
                        mode="promise_in_bounds",
                    )
                    for part in (feature * HALF, feature * HALF + 8)
                ]
                row = feature * chunks + at + side
                picked_ref[row : row + 1, :] = jnp.where(upper, second, first)[:1, :]
    shape = (chunks, LANES)
    chosen = [picked_ref[at * chunks : (at + 1) * chunks, :] for at in range(FEATURES)]

    tile = first_tile + lax.div(iota(shape, 0), per_group) * GROUP + lax.rem(iota(shape, 1), GROUP)
    middle_x = (lax.rem(tile, TILE_COLS) * TILE_SIDE + TILE_SIDE // 2).astype(f32)
    middle_y = (lax.div(tile, TILE_COLS) * TILE_SIDE + TILE_SIDE // 2).astype(f32)
    at_u = chosen[0] - middle_x
    at_v = chosen[1] - middle_y
    conic_a, conic_b, conic_c = chosen[2], chosen[3], chosen[4]
    by_u = conic_a * at_u + conic_b * at_v
    by_v = conic_b * at_u + conic_c * at_v
    coefs = [
        jnp.where(live, log2_e * (chosen[5] - 0.5 * (at_u * by_u + at_v * by_v)), -1e4),
        jnp.where(live, log2_e * by_u, 0.0),
        jnp.where(live, log2_e * by_v, 0.0),
        jnp.where(live, (-0.5 * log2_e) * conic_a, 0.0),
        jnp.where(live, -log2_e * conic_b, 0.0),
        jnp.where(live, (-0.5 * log2_e) * conic_c, 0.0),
    ]
    for at in range(8):
        split = pieces(coefs[at], 3) if at < 6 else [jnp.zeros(shape, bf16)] * 3
        for part in range(3):
            row = (part * 8 + at) * chunks
            coef_ref[row : row + chunks, :] = split[part].astype(f32)
    for at in range(3):
        split = pieces(chosen[6 + at], 3)
        for part in range(3):
            row = (part * 3 + at) * chunks
            color_ref[row : row + chunks, :] = split[part].astype(f32)

    pixel = iota((8, pixels), 1)
    row8 = iota((8, pixels), 0)
    off_x = lax.rem(pixel, TILE_SIDE).astype(f32) - 7.5
    off_y = lax.div(pixel, TILE_SIDE).astype(f32) - 7.5
    base = jnp.where(row8 == 0, 1.0, 0.0)
    for at, values in enumerate([off_x, off_y, off_x * off_x, off_x * off_y, off_y * off_y]):
        base = jnp.where(row8 == at + 1, values, base)
    base_two = jnp.concatenate([base, base], axis=1).astype(bf16)
    base_three = jnp.concatenate([base, base, base], axis=0).astype(bf16)
    same_tile = lax.rem(iota((GROUP, LANES), 1), GROUP) == iota((GROUP, LANES), 0)

    for at in range(chunks):
        rows = []
        for part in range(9):
            row = color_ref[part * chunks + at : part * chunks + at + 1, :]
            rows.append(jnp.where(same_tile, jnp.broadcast_to(row, (GROUP, LANES)), 0.0))
        rows.append(jnp.zeros((GROUP, LANES), f32))
        paint_ref[:, at * LANES : (at + 1) * LANES] = jnp.concatenate(rows, axis=0).astype(bf16)

    def rows_of(chunk, count=1):
        return pl.ds(pl.multiple_of(chunk * LANES, LANES), count * LANES)

    def shade(at, carry):
        coef = jnp.concatenate(
            [coef_ref[pl.ds(at * BLOCK + off, 24, stride=chunks), :] for off in range(BLOCK)], axis=1
        )
        alpha_ref[rows_of(at * BLOCK, BLOCK), :] = jnp.exp2(dot(coef.astype(bf16), base_three, 0, 0))
        return carry

    lax.fori_loop(0, chunks // BLOCK, shade, 0)

    def load(ref, at):
        return [ref[rows_of(group * per_group + at), :] for group in range(groups)]

    def keep(refs, at, made):
        for group in range(groups):
            for ref, values in zip(refs, made[group]):
                ref[rows_of(group * per_group + at), :] = values

    def weigh(at, clears):
        alphas = load(alpha_ref, at)
        out, made = [], []
        for group in range(groups):
            clear, alpha = clears[group], alphas[group]
            weights = []
            for step in range(steps):
                weight = alpha[step * GROUP : (step + 1) * GROUP, :] * clear
                clear = clear - weight
                weights.append(weight)
            weight = jnp.concatenate(weights, axis=0)
            made.append((weight, *pieces(weight, 3)))
            out.append(clear)
        keep((weight_ref, high_ref, middle_ref, low_ref), at, made)
        return tuple(out)

    lax.fori_loop(0, per_group, weigh, (jnp.ones((GROUP, pixels), f32),) * groups)

    def blend(at, renders):
        out = []
        for group in range(groups):
            chunk = group * per_group + at * BLOCK
            rows = rows_of(chunk, BLOCK)
            paint = paint_ref[:72, rows]
            out.append(
                renders[group]
                + (
                    dot(paint, high_ref[rows, :], 1, 0)
                    + (dot(paint, middle_ref[rows, :], 1, 0) + dot(paint, low_ref[rows, :], 1, 0))
                )
            )
        return tuple(out)

    renders = lax.fori_loop(
        0, per_group // BLOCK, blend, (jnp.zeros((72, pixels), f32),) * groups
    )

    signs, sign_twos = [], []
    for group in range(groups):
        render = renders[group]
        render = render[:24] + (render[24:48] + render[48:])
        rows = []
        for at in range(3):
            gap = (
                render[at * GROUP : (at + 1) * GROUP, :]
                - target_ref[at, group * GROUP : (group + 1) * GROUP, :]
            )
            rows.append(jnp.where(gap > 0.0, 1.0, jnp.where(gap < 0.0, -1.0, 0.0)))
        sign = jnp.concatenate(rows, axis=0)
        signs.append(sign.astype(bf16))
        sign_twos.append(jnp.concatenate([sign, sign], axis=0).astype(bf16))

    def draw(at, carry):
        for group in range(groups):
            rows = rows_of(group * per_group + at * BLOCK, BLOCK)
            pull_ref[rows, :] = dot(paint_ref[:48, rows], sign_twos[group], 0, 0)
        return carry

    lax.fori_loop(0, per_group // BLOCK, draw, 0)

    def unweigh(back, behinds):
        at = per_group - 1 - back
        pulls, alphas, weights = [load(ref, at) for ref in (pull_ref, alpha_ref, weight_ref)]
        out, made = [], []
        for group in range(groups):
            pull, alpha, weight = pulls[group], alphas[group], weights[group]
            behind = behinds[group]
            by_alpha = [None] * steps
            for step in reversed(range(steps)):
                part = slice(step * GROUP, (step + 1) * GROUP)
                gap = pull[part, :] - behind
                by_alpha[step] = weight[part, :] * gap
                behind = behind + alpha[part, :] * gap
            made.append(pieces(jnp.concatenate(by_alpha, axis=0), 2))
            out.append(behind)
        keep((low_ref, spread_ref), at, made)
        return tuple(out)

    lax.fori_loop(0, per_group, unweigh, (jnp.zeros((GROUP, pixels), f32),) * groups)

    def total(at, carry):
        for group in range(groups):
            chunk = group * per_group + at * BLOCK
            rows = rows_of(chunk, BLOCK)
            parts = jnp.concatenate([low_ref[rows, :], spread_ref[rows, :]], axis=1)
            moments = dot(base_two, parts, 1, 1)
            by_color = dot(signs[group], high_ref[rows, :], 1, 1)
            for off in range(BLOCK):
                row = pl.multiple_of((chunk + off) * 16, 16)
                lanes = slice(off * LANES, (off + 1) * LANES)
                moment_ref[pl.ds(row, 8), :] = moments[:, lanes]
                for channel in range(3):
                    moment_ref[pl.ds(row + 8 + channel, 1), :] = jnp.sum(
                        jnp.where(
                            same_tile, by_color[channel * GROUP : (channel + 1) * GROUP, lanes], 0.0
                        ),
                        axis=0,
                        keepdims=True,
                    )
        return carry

    lax.fori_loop(0, per_group // BLOCK, total, 0)

    sums = [moment_ref[pl.ds(at, chunks, stride=16), :] for at in range(6)]
    sum_x = sums[1] - at_u * sums[0]
    sum_y = sums[2] - at_v * sums[0]
    sum_xx = sums[3] - 2.0 * at_u * sums[1] + at_u * at_u * sums[0]
    sum_xy = sums[4] - at_u * sums[2] - at_v * sum_x
    sum_yy = sums[5] - 2.0 * at_v * sums[2] + at_v * at_v * sums[0]
    grads = [
        conic_a * sum_x + conic_b * sum_y,
        conic_b * sum_x + conic_c * sum_y,
        -0.5 * sum_xx,
        -sum_xy,
        -0.5 * sum_yy,
        sums[0],
    ] + [moment_ref[pl.ds(8 + at, chunks, stride=16), :] for at in range(3)]

    half_one = small_ids(HALF)
    below = below.astype(f32)
    grads = [pieces(jnp.where(live, grad, 0.0), 2) for grad in grads]
    grads = [[part.astype(f32) for part in split] for split in grads]
    for at in range(chunks):
        mask = one_hot(half_one, below[at : at + 1, :])
        for part in range(2):
            for feature in range(FEATURES):
                row = grads[feature][part][at : at + 1, :]
                grad_ref[
                    part * span + feature * HALF : part * span + (feature + 1) * HALF,
                    at * LANES : (at + 1) * LANES,
                ] = mask * jnp.broadcast_to(row, (HALF, LANES)).astype(bf16)
    sent = dot(grad_ref[...], hot_ref[...], 1, 1)
    sent = sent[:span] + sent[span:]
    sent = jnp.concatenate(
        [sent[:, :LANES], sent[:, LANES:], jnp.zeros((3 * LANES - 2 * span, LANES), f32)], axis=0
    )
    spread_rows(sent, grads_ref)


def tiles_call(entries, rank, hot, rows, target, owned):
    chunks = entries.shape[0]
    pixels = TILE_SIDE * TILE_SIDE
    count = chunks * LANES

    def plane(dtype):
        return pltpu.VMEM((count, pixels), dtype)

    return pl.pallas_call(
        lambda *refs: tile_kernel(owned, *refs),
        out_shape=jax.ShapeDtypeStruct((3 * LANES, LANES), f32),
        scratch_shapes=[
            pltpu.VMEM((FEATURES * chunks, LANES), f32),
            pltpu.VMEM((24 * chunks, LANES), f32),
            pltpu.VMEM((9 * chunks, LANES), f32),
            plane(f32),
            plane(f32),
            plane(bf16),
            plane(bf16),
            plane(bf16),
            plane(f32),
            pltpu.VMEM((16 * chunks, LANES), f32),
            pltpu.VMEM((2 * FEATURES * HALF, count), bf16),
            plane(bf16),
            pltpu.VMEM((80, count), bf16),
        ],
        compiler_params=pltpu.CompilerParams(vmem_limit_bytes=48 * 1024 * 1024),
        name="tiles",
    )(entries, rank, hot, rows, target)


def learning_rates(shape):
    row = iota(shape, 0)
    rates = jnp.full(shape, 0.000125, f32)
    for stop, rate in ((14, 0.0025), (11, 0.05), (10, 0.001), (6, 0.005), (3, 0.00016)):
        rates = jnp.where(row < stop, rate, rates)
    return rates


def update_kernel(
    frame,
    params_ref,
    first_hbm,
    second_hbm,
    cameras_ref,
    asked_ref,
    column_ref,
    grads_ref,
    new_params_ref,
    new_first_ref,
    new_second_ref,
    source_ref,
    spread_ref,
    dense_ref,
    gradient_ref,
    first_ref,
    second_ref,
    arrived,
):
    owned = params_ref.shape[1]
    copies = [
        pltpu.make_async_copy(source, target, arrived.at[at])
        for at, (source, target) in enumerate(((first_hbm, first_ref), (second_hbm, second_ref)))
    ]
    for copy in copies:
        copy.start()
    upper = lax.div(flipped_requests(asked_ref), 2 * LANES)
    key = (lax.div(iota((SLOTS, LANES), 1), LANES // VIEWS) * 2 + upper).astype(f32)
    flipped = gathered_rows(grads_ref)
    for part, values in enumerate(pieces(flipped, 2)):
        source_ref[part * 3 * LANES : (part + 1) * 3 * LANES, :] = values.astype(f32)
    source_ref[6 * LANES :, :] = jnp.zeros((LANES, LANES), f32)
    keys = [jnp.full((16, LANES), at, f32).astype(bf16) for at in range(2 * VIEWS)]
    for slot in range(SLOTS):
        first = slot // HALF * FEATURES * HALF + slot % HALF
        mine = jnp.broadcast_to(key[slot : slot + 1, :], (16, LANES)).astype(bf16)
        parts = [
            source_ref[pl.ds(part * 3 * LANES + first, 16, stride=HALF), :].astype(bf16)
            for part in range(2)
        ]
        spread_ref[:, slot * LANES : (slot + 1) * LANES] = jnp.concatenate(
            [
                jnp.where(mine == keys[at], values, jnp.zeros((), bf16))
                for values in parts
                for at in range(2 * VIEWS)
            ],
            axis=0,
        )
    dense = dot(spread_ref[...], column_ref[...], 1, 1)
    dense = dense[:LANES] + dense[LANES:]
    spans = range(owned // LANES)
    for span in spans:
        side, lanes = span // 2, slice(span % 2 * LANES, (span % 2 + 1) * LANES)
        for view in range(VIEWS):
            row = (view * 2 + side) * 16
            dense_ref[(span * VIEWS + view) * 16 : (span * VIEWS + view + 1) * 16, :] = dense[
                row : row + 16, lanes
            ]
    cotangents = [
        jnp.concatenate(
            [dense_ref[pl.ds(span * VIEWS * 16 + at, VIEWS, stride=16), :] for span in spans], axis=1
        )
        for at in range(FEATURES)
    ]

    rotation, shift = camera_terms(cameras_ref, owned)
    params = [jnp.broadcast_to(params_ref[at : at + 1, :], (VIEWS, owned)) for at in range(59)]
    _, pullback = jax.vjp(lambda values: project(values, rotation, shift, *frame), params)
    by_params = pullback(cotangents)[0]
    for at in range(59):
        gradient_ref[at : at + 1, :] = jnp.sum(by_params[at], axis=0, keepdims=True)
    gradient = gradient_ref[:59, :]
    for copy in copies:
        copy.wait()
    new_first = beta_one * first_ref[...] + (1.0 - beta_one) * gradient
    new_second = beta_two * second_ref[...] + (1.0 - beta_two) * gradient * gradient
    new_first_ref[...] = new_first
    new_second_ref[...] = new_second
    step_size = learning_rates((59, owned)) * (new_first / (1.0 - beta_one**ADAM_STEP))
    new_params_ref[...] = params_ref[...] - step_size / (
        jnp.sqrt(new_second / (1.0 - beta_two**ADAM_STEP)) + adam_eps
    )


def per_device(params, first_moment, second_moment, cameras, target, lists, lengths):
    owned = params.shape[1]
    list_size = lists.shape[2]
    tile_dev = lists.shape[1]
    entry_count = tile_dev * list_size
    chunks = entry_count // LANES
    width = TILE_COLS * TILE_SIDE
    height = tile_dev * lax.axis_size("tiles") // TILE_COLS * TILE_SIDE
    frame = (float(width), 0.5 * width, 0.5 * height)
    limits = pltpu.CompilerParams(vmem_limit_bytes=48 * 1024 * 1024)

    def full(shape, dtype=f32):
        return jax.ShapeDtypeStruct(shape, dtype)

    def sent(rows):
        rows = lax.all_to_all(rows.reshape(LANES, 3 * LANES), AXES, 0, 0, tiled=True)
        return rows.reshape(3 * LANES, LANES)

    entries, rank, requests = pl.pallas_call(
        lambda *refs: rank_kernel(owned, *refs),
        out_shape=(full((chunks, LANES), i32), full((chunks, LANES), i32), full((LANES, SLOTS))),
        scratch_shapes=[
            pltpu.VMEM((LANES, entry_count), bf16),
            pltpu.VMEM((2 * SLOTS, entry_count), bf16),
        ],
        compiler_params=limits,
        name="rank",
    )(lists[0], lengths)
    asked = lax.all_to_all(requests, AXES, 0, 0, tiled=True)
    table = pl.pallas_call(
        lambda *refs: project_kernel(frame, *refs),
        out_shape=full((FEATURES * VIEWS, owned)),
        compiler_params=limits,
        cost_estimate=pl.CostEstimate(flops=4000000, bytes_accessed=200000, transcendentals=20000),
        name="project",
    )(params, cameras)
    answers = pl.pallas_call(
        answer_kernel,
        out_shape=full((3 * LANES, LANES)),
        compiler_params=limits,
        name="answer",
    )(table, asked)
    rows = sent(answers)
    hot, column = pl.pallas_call(
        lambda *refs: prepare_kernel(owned, *refs),
        out_shape=(full((2 * LANES, entry_count), bf16),) * 2,
        compiler_params=limits,
        cost_estimate=pl.CostEstimate(flops=4000000, bytes_accessed=4200000, transcendentals=0),
        name="prepare",
    )(entries, rank, asked)
    row_grads = tiles_call(entries, rank, hot, rows, target[0].transpose(1, 0, 2), owned)
    shares = sent(row_grads)
    whole = pl.BlockSpec(memory_space=pltpu.VMEM)
    away = pl.BlockSpec(memory_space=pl.ANY)
    return pl.pallas_call(
        lambda *refs: update_kernel(frame, *refs),
        out_shape=(full(params.shape),) * 3,
        in_specs=[whole, away, away, whole, whole, whole, whole],
        scratch_shapes=[
            pltpu.VMEM((7 * LANES, LANES), f32),
            pltpu.VMEM((2 * LANES, SLOTS * LANES), bf16),
            pltpu.VMEM((VIEWS * 16 * (owned // LANES), LANES), f32),
            pltpu.VMEM((64, owned), f32),
            pltpu.VMEM(params.shape, f32),
            pltpu.VMEM(params.shape, f32),
            pltpu.SemaphoreType.DMA((2,)),
        ],
        compiler_params=limits,
        name="update",
    )(params, first_moment, second_moment, cameras, asked, column, shares)


def solution(mesh):
    placed = (
        P(None, AXES),
        P(None, AXES),
        P(None, AXES),
        P(),
        P("views", "tiles", None, None),
        P("views", "tiles", None),
        P("views", "tiles"),
    )
    return jax.shard_map(
        per_device,
        mesh=mesh,
        in_specs=placed,
        out_specs=(P(None, AXES),) * 3,
        check_vma=False,
    )
```

```python
import jax
import jax.numpy as jnp
from jax import lax
from jax.experimental import pallas as pl
from jax.experimental.pallas import tpu as pltpu
from jax.sharding import PartitionSpec as P

TILE_SIDE = 16
TILE_COLS = 32
ADAM_STEP = 1000
GROUP = 8
LANES = 128
VIEWS = 4
SLOTS = 32
HALF = SLOTS // 2
KEYS = 2 * VIEWS
PARAMS = 59
TABLE = 80
BLOCK = 4
FEATURES = 9
AXES = ("views", "tiles")

f32 = jnp.float32
bf16 = jnp.bfloat16
i32 = jnp.int32

sh_zero = 0.28209479177387814
sh_first = 0.4886025119029199
sh_second = (
    1.0925484305920792,
    -1.0925484305920792,
    0.31539156525252005,
    -1.0925484305920792,
    0.5462742152960396,
)
sh_third = (
    -0.5900435899266435,
    2.890611442640554,
    -0.4570457994644658,
    0.3731763325901154,
    -0.4570457994644658,
    1.445305721320277,
    -0.5900435899266435,
)
beta_one = 0.9
beta_two = 0.999
adam_eps = 1e-15
log2_e = 1.4426950408889634


def matmul_three(left, right):
    return [
        [
            left[row_at][0] * right[0][col_at]
            + left[row_at][1] * right[1][col_at]
            + left[row_at][2] * right[2][col_at]
            for col_at in range(3)
        ]
        for row_at in range(3)
    ]


def rotation_entries(cos, sin):
    cos_a, cos_b, cos_c = cos
    sin_a, sin_b, sin_c = sin
    return [
        [cos_c * cos_b, cos_c * sin_b * sin_a - sin_c * cos_a, cos_c * sin_b * cos_a + sin_c * sin_a],
        [sin_c * cos_b, sin_c * sin_b * sin_a + cos_c * cos_a, sin_c * sin_b * cos_a - cos_c * sin_a],
        [-sin_b, cos_b * sin_a, cos_b * cos_a],
    ]


def sh_basis(along_x, along_y, along_z):
    square_x, square_y, square_z = (along_x * along_x, along_y * along_y, along_z * along_z)
    both_xy, both_yz, both_xz = (along_x * along_y, along_y * along_z, along_x * along_z)
    return [
        sh_zero + 0.0 * along_x,
        -sh_first * along_y,
        sh_first * along_z,
        -sh_first * along_x,
        sh_second[0] * both_xy,
        sh_second[1] * both_yz,
        sh_second[2] * (2.0 * square_z - square_x - square_y),
        sh_second[3] * both_xz,
        sh_second[4] * (square_x - square_y),
        sh_third[0] * along_y * (3.0 * square_x - square_y),
        sh_third[1] * both_xy * along_z,
        sh_third[2] * along_y * (4.0 * square_z - square_x - square_y),
        sh_third[3] * along_z * (2.0 * square_z - 3.0 * square_x - 3.0 * square_y),
        sh_third[4] * along_x * (4.0 * square_z - square_x - square_y),
        sh_third[5] * along_z * (square_x - square_y),
        sh_third[6] * along_x * (square_x - 3.0 * square_y),
    ]


def project(params, rotation, shift, focal_len, center_x, center_y):
    means = params[:3]
    point = [
        rotation[axis_at][0] * means[0]
        + rotation[axis_at][1] * means[1]
        + rotation[axis_at][2] * means[2]
        + shift[axis_at]
        for axis_at in range(3)
    ]
    inverse_z = 1.0 / point[2]
    screen_u = focal_len * point[0] * inverse_z + center_x
    screen_v = focal_len * point[1] * inverse_z + center_y
    scales = [jnp.exp(params[3 + axis_at]) for axis_at in range(3)]
    quat = params[6:10]
    inverse_norm = lax.rsqrt(
        quat[0] * quat[0] + quat[1] * quat[1] + quat[2] * quat[2] + quat[3] * quat[3]
    )
    real_part, imag_x, imag_y, imag_z = [part * inverse_norm for part in quat]
    spin = [
        [
            1.0 - 2.0 * (imag_y * imag_y + imag_z * imag_z),
            2.0 * (imag_x * imag_y - real_part * imag_z),
            2.0 * (imag_x * imag_z + real_part * imag_y),
        ],
        [
            2.0 * (imag_x * imag_y + real_part * imag_z),
            1.0 - 2.0 * (imag_x * imag_x + imag_z * imag_z),
            2.0 * (imag_y * imag_z - real_part * imag_x),
        ],
        [
            2.0 * (imag_x * imag_z - real_part * imag_y),
            2.0 * (imag_y * imag_z + real_part * imag_x),
            1.0 - 2.0 * (imag_x * imag_x + imag_y * imag_y),
        ],
    ]
    turned = matmul_three(rotation, spin)
    shaped = [
        [turned[row_at][col_at] * scales[col_at] for col_at in range(3)] for row_at in range(3)
    ]
    near_x = [
        focal_len * inverse_z * shaped[0][col_at]
        - focal_len * point[0] * inverse_z * inverse_z * shaped[2][col_at]
        for col_at in range(3)
    ]
    near_y = [
        focal_len * inverse_z * shaped[1][col_at]
        - focal_len * point[1] * inverse_z * inverse_z * shaped[2][col_at]
        for col_at in range(3)
    ]
    cov_a = near_x[0] * near_x[0] + near_x[1] * near_x[1] + near_x[2] * near_x[2] + 0.3
    cov_b = near_x[0] * near_y[0] + near_x[1] * near_y[1] + near_x[2] * near_y[2]
    cov_c = near_y[0] * near_y[0] + near_y[1] * near_y[1] + near_y[2] * near_y[2] + 0.3
    determinant = cov_a * cov_c - cov_b * cov_b
    offset = [
        means[axis_at]
        + rotation[0][axis_at] * shift[0]
        + rotation[1][axis_at] * shift[1]
        + rotation[2][axis_at] * shift[2]
        for axis_at in range(3)
    ]
    inverse_len = lax.rsqrt(offset[0] * offset[0] + offset[1] * offset[1] + offset[2] * offset[2])
    basis = sh_basis(offset[0] * inverse_len, offset[1] * inverse_len, offset[2] * inverse_len)
    colors = [
        0.5 + sum((basis[coef_at] * params[11 + 3 * coef_at + channel] for coef_at in range(16)))
        for channel in range(3)
    ]
    log_opacity = params[10] - jnp.log1p(jnp.exp(params[10]))
    return [
        screen_u,
        screen_v,
        cov_c / determinant,
        -cov_b / determinant,
        cov_a / determinant,
        log_opacity,
        colors[0],
        colors[1],
        colors[2],
    ]


def both_halves(upper, lower):
    return jnp.concatenate([upper, lower], axis=0)


def camera_terms(cameras_ref, half):
    cameras = cameras_ref[...]
    cos, sin = jnp.cos(cameras), jnp.sin(cameras)

    def column(values, at):
        values = values[:, at : at + 1]
        return jnp.broadcast_to(both_halves(values, values), (KEYS, half))

    rotation = rotation_entries(
        [column(cos, at) for at in range(3)], [column(sin, at) for at in range(3)]
    )
    return rotation, [column(cameras, 3 + at) for at in range(3)]


def spread_params(params_ref, half):
    return [
        both_halves(
            jnp.broadcast_to(params_ref[at : at + 1, :half], (VIEWS, half)),
            jnp.broadcast_to(params_ref[at : at + 1, half:], (VIEWS, half)),
        )
        for at in range(PARAMS)
    ]


def iota(shape, dim):
    return lax.broadcasted_iota(i32, shape, dim)


def dot(left, right, left_dim, right_dim):
    return lax.dot_general(
        left, right, (((left_dim,), (right_dim,)), ((), ())), preferred_element_type=f32
    )


def pieces(values, count):
    out = []
    for at in range(count):
        part = values.astype(bf16)
        out.append(part)
        if at + 1 < count:
            values = values - part.astype(f32)
    return out


def one_hot(ids, row):
    row = jnp.broadcast_to(row, (16, row.shape[1])).astype(bf16)
    row = jnp.concatenate([row] * (ids.shape[0] // 16), axis=0)
    return jnp.where(ids == row, jnp.ones((), bf16), jnp.zeros((), bf16))


def small_ids(count):
    return iota((count, LANES), 0).astype(f32).astype(bf16)


def rank_kernel(
    owned, lists_ref, entries_ref, rank_ref, request_ref, hot_ref, wanted_ref
):
    chunks = entries_ref.shape[0]
    per_group = chunks // 2
    steps = LANES // GROUP
    lane = iota((GROUP, LANES), 1)
    tile = lax.rem(lane, GROUP)
    spot = iota((GROUP, LANES), 0) * steps + lax.div(lane, GROUP)
    for group in range(2):
        for half in range(per_group // GROUP):
            made = jnp.zeros((GROUP, LANES), i32)
            for at in range(GROUP):
                row = group * GROUP + at
                source = jnp.broadcast_to(
                    lists_ref[row : row + 1, half * LANES : (half + 1) * LANES], (GROUP, LANES)
                )
                found = jnp.take_along_axis(source, spot, axis=1, mode="promise_in_bounds")
                made = jnp.where(tile == at, found, made)
            row = group * per_group + half * GROUP
            entries_ref[row : row + GROUP, :] = made
    entries = entries_ref[...]
    owner = lax.div(entries, owned)
    owner_row = owner.astype(f32)
    column = lax.rem(entries, owned)
    low = lax.rem(column, 256).astype(f32)
    high = lax.div(column, 256).astype(f32)
    before = jnp.where(iota((LANES, LANES), 0) < iota((LANES, LANES), 1), 1.0, 0.0)
    adder = jnp.concatenate([before, jnp.ones((LANES, LANES), f32)], axis=1).astype(bf16)
    owner_id = iota((LANES, LANES), 0)
    owner_one = small_ids(LANES)
    slot_one = small_ids(SLOTS)
    base = jnp.zeros((LANES, LANES), f32)
    for at in range(chunks):
        lanes = slice(at * LANES, (at + 1) * LANES)
        hot = one_hot(owner_one, owner_row[at : at + 1, :])
        hot_ref[:, lanes] = hot
        counts = dot(hot, adder, 1, 0)
        rank = jnp.sum(
            jnp.where(owner_id == owner[at : at + 1, :], counts[:, :LANES] + base, 0.0),
            axis=0,
            keepdims=True,
        )
        base = base + counts[:, LANES:]
        rank_ref[at : at + 1, :] = rank.astype(i32)
        slot = one_hot(slot_one, rank)
        wanted_ref[:, lanes] = jnp.concatenate(
            [
                slot * jnp.broadcast_to(part[at : at + 1, :], (SLOTS, LANES)).astype(bf16)
                for part in (low, high)
            ],
            axis=0,
        )
    requests = dot(hot_ref[...], wanted_ref[...], 1, 1)
    request_ref[...] = requests[:, :SLOTS] + 256.0 * requests[:, SLOTS:]


def flipped_requests(asked_ref):
    asked = asked_ref[...]
    wide = jnp.concatenate([asked, jnp.zeros((LANES, LANES - SLOTS), f32)], axis=1)
    return wide.T[:SLOTS, :].astype(i32)


def project_kernel(frame, params_ref, cameras_ref, table_ref):
    half = params_ref.shape[1] // 2
    rotation, shift = camera_terms(cameras_ref, half)
    rows = project(spread_params(params_ref, half), rotation, shift, *frame)
    rows.append(jnp.zeros((TABLE - FEATURES * KEYS, half), f32))
    for part, values in enumerate(pieces(jnp.concatenate(rows, axis=0), 3)):
        table_ref[part * TABLE : (part + 1) * TABLE, :] = values


def request_keys(asked):
    half = 2 * LANES
    return lax.div(asked, half) * VIEWS + lax.div(iota(asked.shape, 1), LANES // VIEWS)


def spread_rows(stack, out_ref):
    for part in range(3):
        out_ref[pl.ds(part, LANES, stride=3), :] = stack[part * LANES : (part + 1) * LANES].T


def gathered_rows(rows_ref):
    return jnp.concatenate(
        [rows_ref[pl.ds(part, LANES, stride=3), :].T for part in range(3)], axis=0
    )


def pick_sublane(values, row):
    index = jnp.broadcast_to(row, (8, values.shape[1]))
    return jnp.take_along_axis(values, index, axis=0, mode="promise_in_bounds")


def fill_columns(asked, column_ref):
    low = lax.rem(asked, 2 * LANES).astype(f32)
    ids = small_ids(2 * LANES)
    for at in range(SLOTS):
        column_ref[:, at * LANES : (at + 1) * LANES] = one_hot(ids, low[at : at + 1, :])


def answer_kernel(table_ref, asked_ref, rows_ref, column_ref, stack_ref):
    asked = flipped_requests(asked_ref)
    key = request_keys(asked)
    fill_columns(asked, column_ref)
    table = table_ref[...]
    for at in range(0, SLOTS, 2):
        found = dot(table, column_ref[:, at * LANES : (at + 2) * LANES], 1, 0)
        found = found[:TABLE] + (found[TABLE : 2 * TABLE] + found[2 * TABLE :])
        for side in range(2):
            slot = at + side
            for feature in range(FEATURES):
                row = slot // HALF * FEATURES * HALF + feature * HALF + slot % HALF
                stack_ref[row : row + 1, :] = pick_sublane(
                    found[feature * KEYS : (feature + 1) * KEYS, side * LANES : (side + 1) * LANES],
                    key[slot : slot + 1, :],
                )[:1, :]
    stack_ref[SLOTS * FEATURES :, :] = jnp.zeros((3 * LANES - SLOTS * FEATURES, LANES), f32)
    spread_rows(stack_ref[...], rows_ref)


def prepare_kernel(
    owned,
    entries_ref,
    rank_ref,
    lengths_ref,
    target_ref,
    first_ref,
    second_ref,
    asked_ref,
    hot_ref,
    column_ref,
    live_ref,
    aim_ref,
    old_first_ref,
    old_second_ref,
):
    fill_columns(flipped_requests(asked_ref), column_ref)
    old_first_ref[...] = beta_one * first_ref[...]
    old_second_ref[...] = beta_two * second_ref[...]
    ids = small_ids(2 * LANES)
    place, _ = slot_columns(entries_ref[...], rank_ref[...], owned)
    place = place.astype(f32)
    for at in range(entries_ref.shape[0]):
        hot_ref[:, at * LANES : (at + 1) * LANES] = one_hot(ids, place[at : at + 1, :])
    lengths = jnp.concatenate(
        [lengths_ref[...], jnp.zeros((1, LANES - lengths_ref.shape[1]), i32)], axis=1
    )
    shape = entries_ref.shape
    per_group = shape[0] // 2
    tile = lax.div(iota(shape, 0), per_group) * GROUP + lax.rem(iota(shape, 1), GROUP)
    length = jnp.take_along_axis(
        jnp.broadcast_to(lengths, shape), tile, axis=1, mode="promise_in_bounds"
    )
    steps = LANES // GROUP
    spot = lax.rem(iota(shape, 0), per_group) * steps + lax.div(iota(shape, 1), GROUP)
    live_ref[...] = jnp.where(spot < length, 1, 0)
    aim_ref[...] = target_ref[...]


def slot_columns(entries, rank, owned):
    owner = lax.div(entries, owned)
    return lax.div(rank, HALF) * LANES + owner, lax.rem(rank, HALF)


def tile_kernel(
    live_ref,
    rank_ref,
    hot_ref,
    rows_ref,
    target_ref,
    grads_ref,
    picked_ref,
    coef_ref,
    color_ref,
    alpha_ref,
    weight_ref,
    high_ref,
    middle_ref,
    low_ref,
    pull_ref,
    moment_ref,
    grad_ref,
    spread_ref,
    paint_ref,
):
    chunks = live_ref.shape[0]
    groups = 2
    per_group = chunks // groups
    pixels = TILE_SIDE * TILE_SIDE
    steps = LANES // GROUP
    span = FEATURES * HALF
    first_tile = lax.axis_index("tiles") * (groups * GROUP)

    live = live_ref[...] > 0
    below = lax.rem(rank_ref[...], HALF)

    flipped = gathered_rows(rows_ref)
    table = jnp.concatenate([flipped[:span], flipped[span : 2 * span]], axis=1)
    table = jnp.concatenate(pieces(table, 3), axis=0)
    for at in range(0, chunks, 2):
        found = dot(table, hot_ref[:, at * LANES : (at + 2) * LANES], 1, 0)
        found = found[:span] + (found[span : 2 * span] + found[2 * span :])
        for side in range(2):
            row = below[at + side : at + side + 1, :]
            index, upper = lax.rem(row, 8), jnp.broadcast_to(row, (8, LANES)) >= 8
            for feature in range(FEATURES):
                first, second = [
                    pick_sublane(
                        found[part : part + 8, side * LANES : (side + 1) * LANES], index
                    )
                    for part in (feature * HALF, feature * HALF + 8)
                ]
                row = feature * chunks + at + side
                picked_ref[row : row + 1, :] = jnp.where(upper, second, first)[:1, :]
    shape = (chunks, LANES)
    chosen = [picked_ref[at * chunks : (at + 1) * chunks, :] for at in range(FEATURES)]

    tile = first_tile + lax.div(iota(shape, 0), per_group) * GROUP + lax.rem(iota(shape, 1), GROUP)
    middle_x = (lax.rem(tile, TILE_COLS) * TILE_SIDE + TILE_SIDE // 2).astype(f32)
    middle_y = (lax.div(tile, TILE_COLS) * TILE_SIDE + TILE_SIDE // 2).astype(f32)
    at_u = chosen[0] - middle_x
    at_v = chosen[1] - middle_y
    conic_a, conic_b, conic_c = chosen[2], chosen[3], chosen[4]
    by_u = conic_a * at_u + conic_b * at_v
    by_v = conic_b * at_u + conic_c * at_v
    coefs = [
        jnp.where(live, log2_e * (chosen[5] - 0.5 * (at_u * by_u + at_v * by_v)), -1e4),
        jnp.where(live, log2_e * by_u, 0.0),
        jnp.where(live, log2_e * by_v, 0.0),
        jnp.where(live, (-0.5 * log2_e) * conic_a, 0.0),
        jnp.where(live, -log2_e * conic_b, 0.0),
        jnp.where(live, (-0.5 * log2_e) * conic_c, 0.0),
    ]
    for at in range(8):
        split = pieces(coefs[at], 3) if at < 6 else [jnp.zeros(shape, bf16)] * 3
        for part in range(3):
            row = (part * 8 + at) * chunks
            coef_ref[row : row + chunks, :] = split[part].astype(f32)
    for at in range(3):
        split = pieces(chosen[6 + at], 3)
        for part in range(3):
            row = (part * 3 + at) * chunks
            color_ref[row : row + chunks, :] = split[part].astype(f32)

    pixel = iota((8, pixels), 1)
    row8 = iota((8, pixels), 0)
    off_x = lax.rem(pixel, TILE_SIDE).astype(f32) - 7.5
    off_y = lax.div(pixel, TILE_SIDE).astype(f32) - 7.5
    base = jnp.where(row8 == 0, 1.0, 0.0)
    for at, values in enumerate([off_x, off_y, off_x * off_x, off_x * off_y, off_y * off_y]):
        base = jnp.where(row8 == at + 1, values, base)
    base_two = jnp.concatenate([base, base], axis=1).astype(bf16)
    base_three = jnp.concatenate([base, base, base], axis=0).astype(bf16)
    same_tile = lax.rem(iota((GROUP, LANES), 1), GROUP) == iota((GROUP, LANES), 0)

    for at in range(chunks):
        rows = []
        for part in range(9):
            row = color_ref[part * chunks + at : part * chunks + at + 1, :]
            rows.append(jnp.where(same_tile, jnp.broadcast_to(row, (GROUP, LANES)), 0.0))
        rows.append(jnp.zeros((GROUP, LANES), f32))
        paint_ref[:, at * LANES : (at + 1) * LANES] = jnp.concatenate(rows, axis=0).astype(bf16)

    def rows_of(chunk, count=1):
        return slice(chunk * LANES, (chunk + count) * LANES)

    blocks = per_group // BLOCK

    def shade(at):
        for group in range(groups):
            chunk = group * per_group + at * BLOCK
            coef = jnp.concatenate(
                [coef_ref[pl.ds(chunk + off, 24, stride=chunks), :] for off in range(BLOCK)], axis=1
            )
            alpha_ref[rows_of(chunk, BLOCK), :] = jnp.exp2(
                dot(coef.astype(bf16), base_three, 0, 0)
            )

    def load(ref, at):
        return [ref[rows_of(group * per_group + at), :] for group in range(groups)]

    def keep(refs, at, made):
        for group in range(groups):
            for ref, values in zip(refs, made[group]):
                ref[rows_of(group * per_group + at), :] = values

    def weigh(at, clears):
        alphas = load(alpha_ref, at)
        out, made = [], []
        for group in range(groups):
            clear, alpha = clears[group], alphas[group]
            weights = []
            for step in range(steps):
                weight = alpha[step * GROUP : (step + 1) * GROUP, :] * clear
                clear = clear - weight
                weights.append(weight)
            weight = jnp.concatenate(weights, axis=0)
            made.append((weight, *pieces(weight, 3)))
            out.append(clear)
        keep((weight_ref, high_ref, middle_ref, low_ref), at, made)
        return tuple(out)

    def blend(at, renders):
        out = []
        for group in range(groups):
            chunk = group * per_group + at * BLOCK
            rows = rows_of(chunk, BLOCK)
            paint = paint_ref[:72, rows]
            out.append(
                renders[group]
                + (
                    dot(paint, high_ref[rows, :], 1, 0)
                    + (dot(paint, middle_ref[rows, :], 1, 0) + dot(paint, low_ref[rows, :], 1, 0))
                )
            )
        return tuple(out)

    clears = (jnp.ones((GROUP, pixels), f32),) * groups
    renders = (jnp.zeros((72, pixels), f32),) * groups
    shade(0)
    for block in range(blocks):
        if block + 1 < blocks:
            shade(block + 1)
        for at in range(block * BLOCK, (block + 1) * BLOCK):
            clears = weigh(at, clears)
        renders = blend(block, renders)

    signs, sign_twos = [], []
    for group in range(groups):
        render = renders[group]
        render = render[:24] + (render[24:48] + render[48:])
        rows = []
        for at in range(3):
            gap = (
                render[at * GROUP : (at + 1) * GROUP, :]
                - target_ref[at, group * GROUP : (group + 1) * GROUP, :]
            )
            rows.append(jnp.where(gap > 0.0, 1.0, jnp.where(gap < 0.0, -1.0, 0.0)))
        sign = jnp.concatenate(rows, axis=0)
        signs.append(sign.astype(bf16))
        sign_twos.append(jnp.concatenate([sign, sign], axis=0).astype(bf16))

    def draw(at):
        for group in range(groups):
            rows = rows_of(group * per_group + at * BLOCK, BLOCK)
            pull_ref[rows, :] = dot(paint_ref[:48, rows], sign_twos[group], 0, 0)

    def unweigh(at, behinds):
        pulls, alphas, weights = [load(ref, at) for ref in (pull_ref, alpha_ref, weight_ref)]
        out, made = [], []
        for group in range(groups):
            pull, alpha, weight = pulls[group], alphas[group], weights[group]
            behind = behinds[group]
            by_alpha = [None] * steps
            for step in reversed(range(steps)):
                part = slice(step * GROUP, (step + 1) * GROUP)
                gap = pull[part, :] - behind
                by_alpha[step] = weight[part, :] * gap
                behind = behind + alpha[part, :] * gap
            made.append(pieces(jnp.concatenate(by_alpha, axis=0), 2))
            out.append(behind)
        keep((low_ref, spread_ref), at, made)
        return tuple(out)

    def total(at):
        for group in range(groups):
            chunk = group * per_group + at * BLOCK
            rows = rows_of(chunk, BLOCK)
            parts = jnp.concatenate([low_ref[rows, :], spread_ref[rows, :]], axis=1)
            moments = dot(base_two, parts, 1, 1)
            by_color = dot(signs[group], high_ref[rows, :], 1, 1)
            for off in range(BLOCK):
                row = (chunk + off) * 16
                lanes = slice(off * LANES, (off + 1) * LANES)
                moment_ref[pl.ds(row, 8), :] = moments[:, lanes]
                for channel in range(3):
                    moment_ref[pl.ds(row + 8 + channel, 1), :] = jnp.sum(
                        jnp.where(
                            same_tile, by_color[channel * GROUP : (channel + 1) * GROUP, lanes], 0.0
                        ),
                        axis=0,
                        keepdims=True,
                    )

    behinds = (jnp.zeros((GROUP, pixels), f32),) * groups
    draw(blocks - 1)
    for block in reversed(range(blocks)):
        if block:
            draw(block - 1)
        for at in reversed(range(block * BLOCK, (block + 1) * BLOCK)):
            behinds = unweigh(at, behinds)
        total(block)

    sums = [moment_ref[pl.ds(at, chunks, stride=16), :] for at in range(6)]
    sum_x = sums[1] - at_u * sums[0]
    sum_y = sums[2] - at_v * sums[0]
    sum_xx = sums[3] - 2.0 * at_u * sums[1] + at_u * at_u * sums[0]
    sum_xy = sums[4] - at_u * sums[2] - at_v * sum_x
    sum_yy = sums[5] - 2.0 * at_v * sums[2] + at_v * at_v * sums[0]
    grads = [
        conic_a * sum_x + conic_b * sum_y,
        conic_b * sum_x + conic_c * sum_y,
        -0.5 * sum_xx,
        -sum_xy,
        -0.5 * sum_yy,
        sums[0],
    ] + [moment_ref[pl.ds(8 + at, chunks, stride=16), :] for at in range(3)]

    half_one = small_ids(HALF)
    below = below.astype(f32)
    grads = [pieces(jnp.where(live, grad, 0.0), 2) for grad in grads]
    grads = [[part.astype(f32) for part in split] for split in grads]
    for at in range(chunks):
        mask = one_hot(half_one, below[at : at + 1, :])
        for part in range(2):
            for feature in range(FEATURES):
                row = grads[feature][part][at : at + 1, :]
                grad_ref[
                    part * span + feature * HALF : part * span + (feature + 1) * HALF,
                    at * LANES : (at + 1) * LANES,
                ] = mask * jnp.broadcast_to(row, (HALF, LANES)).astype(bf16)
    sent = dot(grad_ref[...], hot_ref[...], 1, 1)
    sent = sent[:span] + sent[span:]
    sent = jnp.concatenate(
        [sent[:, :LANES], sent[:, LANES:], jnp.zeros((3 * LANES - 2 * span, LANES), f32)], axis=0
    )
    spread_rows(sent, grads_ref)


def tiles_call(live, rank, hot, rows, target):
    chunks = live.shape[0]
    pixels = TILE_SIDE * TILE_SIDE
    count = chunks * LANES

    def plane(dtype):
        return pltpu.VMEM((count, pixels), dtype)

    return pl.pallas_call(
        tile_kernel,
        out_shape=jax.ShapeDtypeStruct((3 * LANES, LANES), f32),
        scratch_shapes=[
            pltpu.VMEM((FEATURES * chunks, LANES), f32),
            pltpu.VMEM((24 * chunks, LANES), f32),
            pltpu.VMEM((9 * chunks, LANES), f32),
            plane(f32),
            plane(f32),
            plane(bf16),
            plane(bf16),
            plane(bf16),
            plane(f32),
            pltpu.VMEM((16 * chunks, LANES), f32),
            pltpu.VMEM((2 * FEATURES * HALF, count), bf16),
            plane(bf16),
            pltpu.VMEM((80, count), bf16),
        ],
        compiler_params=pltpu.CompilerParams(vmem_limit_bytes=32 * 1024 * 1024),
        name="tiles",
    )(live, rank, hot, rows, target)


def learning_rates(shape):
    row = iota(shape, 0)
    rates = jnp.full(shape, 0.000125, f32)
    for stop, rate in ((14, 0.0025), (11, 0.05), (10, 0.001), (6, 0.005), (3, 0.00016)):
        rates = jnp.where(row < stop, rate, rates)
    return rates


def update_kernel(
    frame,
    params_ref,
    old_first_ref,
    old_second_ref,
    cameras_ref,
    asked_ref,
    column_ref,
    grads_ref,
    new_params_ref,
    new_first_ref,
    new_second_ref,
    source_ref,
    spread_ref,
    gradient_ref,
):
    owned = params_ref.shape[1]
    half = owned // 2
    key = request_keys(flipped_requests(asked_ref))
    flipped = gathered_rows(grads_ref)
    for part, values in enumerate(pieces(flipped, 2)):
        source_ref[part * 3 * LANES : (part + 1) * 3 * LANES, :] = values.astype(f32)
    key_id = iota((KEYS, LANES), 0)
    for slot in range(SLOTS):
        first = slot // HALF * FEATURES * HALF + slot % HALF
        mine = key_id == key[slot : slot + 1, :]
        rows = []
        for part in range(2):
            for feature in range(FEATURES):
                at = part * 3 * LANES + first + feature * HALF
                row = jnp.broadcast_to(source_ref[at : at + 1, :], (KEYS, LANES))
                rows.append(jnp.where(mine, row, 0.0))
        spread_ref[:, slot * LANES : (slot + 1) * LANES] = jnp.concatenate(rows, axis=0).astype(bf16)
    dense = dot(spread_ref[...], column_ref[...], 1, 1)
    dense = dense[: FEATURES * KEYS] + dense[FEATURES * KEYS :]
    cotangents = [dense[at * KEYS : (at + 1) * KEYS] for at in range(FEATURES)]

    rotation, shift = camera_terms(cameras_ref, half)
    params = spread_params(params_ref, half)
    _, pullback = jax.vjp(lambda values: project(values, rotation, shift, *frame), params)
    by_params = pullback(cotangents)[0]
    for at in range(PARAMS):
        pair = by_params[at] + pltpu.roll(by_params[at], 1, 0)
        four = pair + pltpu.roll(pair, 2, 0)
        gradient_ref[at : at + 1, :half] = four[VIEWS - 1 : VIEWS]
        gradient_ref[at : at + 1, half:] = four[KEYS - 1 :]
    gradient = gradient_ref[:PARAMS, :]
    new_first = old_first_ref[...] + (1.0 - beta_one) * gradient
    new_second = old_second_ref[...] + (1.0 - beta_two) * gradient * gradient
    new_first_ref[...] = new_first
    new_second_ref[...] = new_second
    step_size = learning_rates((PARAMS, owned)) * (new_first / (1.0 - beta_one**ADAM_STEP))
    new_params_ref[...] = params_ref[...] - step_size / (
        jnp.sqrt(new_second / (1.0 - beta_two**ADAM_STEP)) + adam_eps
    )


def per_device(params, first_moment, second_moment, cameras, target, lists, lengths):
    owned = params.shape[1]
    list_size = lists.shape[2]
    tile_dev = lists.shape[1]
    entry_count = tile_dev * list_size
    chunks = entry_count // LANES
    width = TILE_COLS * TILE_SIDE
    height = tile_dev * lax.axis_size("tiles") // TILE_COLS * TILE_SIDE
    frame = (float(width), 0.5 * width, 0.5 * height)
    limits = pltpu.CompilerParams(vmem_limit_bytes=16 * 1024 * 1024)

    def full(shape, dtype=f32):
        return jax.ShapeDtypeStruct(shape, dtype)

    def sent(rows):
        rows = lax.all_to_all(rows.reshape(LANES, 3 * LANES), AXES, 0, 0, tiled=True)
        return rows.reshape(3 * LANES, LANES)

    entries, rank, requests = pl.pallas_call(
        lambda *refs: rank_kernel(owned, *refs),
        out_shape=(full((chunks, LANES), i32), full((chunks, LANES), i32), full((LANES, SLOTS))),
        scratch_shapes=[
            pltpu.VMEM((LANES, entry_count), bf16),
            pltpu.VMEM((2 * SLOTS, entry_count), bf16),
        ],
        compiler_params=limits,
        name="rank",
    )(lists[0])
    asked = lax.all_to_all(requests, AXES, 0, 0, tiled=True)
    table = pl.pallas_call(
        lambda *refs: project_kernel(frame, *refs),
        out_shape=full((3 * TABLE, owned // 2), bf16),
        compiler_params=limits,
        cost_estimate=pl.CostEstimate(flops=4000000, bytes_accessed=200000, transcendentals=20000),
        name="project",
    )(params, cameras)
    columns = (owned // 2, SLOTS * LANES)
    answers = pl.pallas_call(
        answer_kernel,
        out_shape=full((3 * LANES, LANES)),
        scratch_shapes=[pltpu.VMEM(columns, bf16), pltpu.VMEM((3 * LANES, LANES), f32)],
        compiler_params=limits,
        name="answer",
    )(table, asked)
    rows = sent(answers)
    aim = target[0].transpose(1, 0, 2)
    hot, column, live, aim, old_first, old_second = pl.pallas_call(
        lambda *refs: prepare_kernel(owned, *refs),
        out_shape=(
            full((2 * LANES, entry_count), bf16),
            full(columns, bf16),
            full((chunks, LANES), i32),
            full(aim.shape),
            full(params.shape),
            full(params.shape),
        ),
        compiler_params=limits,
        cost_estimate=pl.CostEstimate(flops=4000000, bytes_accessed=2200000, transcendentals=0),
        name="prepare",
    )(entries, rank, lengths, aim, first_moment, second_moment, asked)
    row_grads = tiles_call(live, rank, hot, rows, aim)
    shares = sent(row_grads)
    return pl.pallas_call(
        lambda *refs: update_kernel(frame, *refs),
        out_shape=(full(params.shape),) * 3,
        scratch_shapes=[
            pltpu.VMEM((6 * LANES, LANES), f32),
            pltpu.VMEM((2 * FEATURES * KEYS, SLOTS * LANES), bf16),
            pltpu.VMEM((64, owned), f32),
        ],
        compiler_params=limits,
        name="update",
    )(params, old_first, old_second, cameras, asked, column, shares)


def solution(mesh):
    placed = (
        P(None, AXES),
        P(None, AXES),
        P(None, AXES),
        P(),
        P("views", "tiles", None, None),
        P("views", "tiles", None),
        P("views", "tiles"),
    )
    return jax.shard_map(
        per_device,
        mesh=mesh,
        in_specs=placed,
        out_specs=(P(None, AXES),) * 3,
        check_vma=False,
    )
```

```python
import jax
import jax.numpy as jnp
from jax import lax
from jax.experimental import pallas as pl
from jax.experimental.pallas import tpu as pltpu
from jax.sharding import PartitionSpec as P

TILE_SIDE = 16
TILE_COLS = 32
ADAM_STEP = 1000
GROUP = 8
LANES = 128
VIEWS = 4
SLOTS = 32
HALF = SLOTS // 2
KEYS = 2 * VIEWS
PARAMS = 59
TABLE = 80
BLOCKS = ((0, 4), (4, 4), (8, 4), (12, 4))
FEATURES = 9
AXES = ("views", "tiles")

f32 = jnp.float32
bf16 = jnp.bfloat16
i32 = jnp.int32

sh_zero = 0.28209479177387814
sh_first = 0.4886025119029199
sh_second = (
    1.0925484305920792,
    -1.0925484305920792,
    0.31539156525252005,
    -1.0925484305920792,
    0.5462742152960396,
)
sh_third = (
    -0.5900435899266435,
    2.890611442640554,
    -0.4570457994644658,
    0.3731763325901154,
    -0.4570457994644658,
    1.445305721320277,
    -0.5900435899266435,
)
beta_one = 0.9
beta_two = 0.999
adam_eps = 1e-15
log2_e = 1.4426950408889634


def matmul_three(left, right):
    return [
        [
            left[row_at][0] * right[0][col_at]
            + left[row_at][1] * right[1][col_at]
            + left[row_at][2] * right[2][col_at]
            for col_at in range(3)
        ]
        for row_at in range(3)
    ]


def rotation_entries(cos, sin):
    cos_a, cos_b, cos_c = cos
    sin_a, sin_b, sin_c = sin
    return [
        [cos_c * cos_b, cos_c * sin_b * sin_a - sin_c * cos_a, cos_c * sin_b * cos_a + sin_c * sin_a],
        [sin_c * cos_b, sin_c * sin_b * sin_a + cos_c * cos_a, sin_c * sin_b * cos_a - cos_c * sin_a],
        [-sin_b, cos_b * sin_a, cos_b * cos_a],
    ]


def sh_basis(along_x, along_y, along_z):
    square_x, square_y, square_z = (along_x * along_x, along_y * along_y, along_z * along_z)
    both_xy, both_yz, both_xz = (along_x * along_y, along_y * along_z, along_x * along_z)
    return [
        sh_zero + 0.0 * along_x,
        -sh_first * along_y,
        sh_first * along_z,
        -sh_first * along_x,
        sh_second[0] * both_xy,
        sh_second[1] * both_yz,
        sh_second[2] * (2.0 * square_z - square_x - square_y),
        sh_second[3] * both_xz,
        sh_second[4] * (square_x - square_y),
        sh_third[0] * along_y * (3.0 * square_x - square_y),
        sh_third[1] * both_xy * along_z,
        sh_third[2] * along_y * (4.0 * square_z - square_x - square_y),
        sh_third[3] * along_z * (2.0 * square_z - 3.0 * square_x - 3.0 * square_y),
        sh_third[4] * along_x * (4.0 * square_z - square_x - square_y),
        sh_third[5] * along_z * (square_x - square_y),
        sh_third[6] * along_x * (square_x - 3.0 * square_y),
    ]


def project(params, rotation, shift, focal_len, center_x, center_y):
    means = params[:3]
    point = [
        rotation[axis_at][0] * means[0]
        + rotation[axis_at][1] * means[1]
        + rotation[axis_at][2] * means[2]
        + shift[axis_at]
        for axis_at in range(3)
    ]
    inverse_z = 1.0 / point[2]
    screen_u = focal_len * point[0] * inverse_z + center_x
    screen_v = focal_len * point[1] * inverse_z + center_y
    scales = [jnp.exp(params[3 + axis_at]) for axis_at in range(3)]
    quat = params[6:10]
    inverse_norm = lax.rsqrt(
        quat[0] * quat[0] + quat[1] * quat[1] + quat[2] * quat[2] + quat[3] * quat[3]
    )
    real_part, imag_x, imag_y, imag_z = [part * inverse_norm for part in quat]
    spin = [
        [
            1.0 - 2.0 * (imag_y * imag_y + imag_z * imag_z),
            2.0 * (imag_x * imag_y - real_part * imag_z),
            2.0 * (imag_x * imag_z + real_part * imag_y),
        ],
        [
            2.0 * (imag_x * imag_y + real_part * imag_z),
            1.0 - 2.0 * (imag_x * imag_x + imag_z * imag_z),
            2.0 * (imag_y * imag_z - real_part * imag_x),
        ],
        [
            2.0 * (imag_x * imag_z - real_part * imag_y),
            2.0 * (imag_y * imag_z + real_part * imag_x),
            1.0 - 2.0 * (imag_x * imag_x + imag_y * imag_y),
        ],
    ]
    turned = matmul_three(rotation, spin)
    shaped = [
        [turned[row_at][col_at] * scales[col_at] for col_at in range(3)] for row_at in range(3)
    ]
    near_x = [
        focal_len * inverse_z * shaped[0][col_at]
        - focal_len * point[0] * inverse_z * inverse_z * shaped[2][col_at]
        for col_at in range(3)
    ]
    near_y = [
        focal_len * inverse_z * shaped[1][col_at]
        - focal_len * point[1] * inverse_z * inverse_z * shaped[2][col_at]
        for col_at in range(3)
    ]
    cov_a = near_x[0] * near_x[0] + near_x[1] * near_x[1] + near_x[2] * near_x[2] + 0.3
    cov_b = near_x[0] * near_y[0] + near_x[1] * near_y[1] + near_x[2] * near_y[2]
    cov_c = near_y[0] * near_y[0] + near_y[1] * near_y[1] + near_y[2] * near_y[2] + 0.3
    determinant = cov_a * cov_c - cov_b * cov_b
    offset = [
        means[axis_at]
        + rotation[0][axis_at] * shift[0]
        + rotation[1][axis_at] * shift[1]
        + rotation[2][axis_at] * shift[2]
        for axis_at in range(3)
    ]
    inverse_len = lax.rsqrt(offset[0] * offset[0] + offset[1] * offset[1] + offset[2] * offset[2])
    basis = sh_basis(offset[0] * inverse_len, offset[1] * inverse_len, offset[2] * inverse_len)
    colors = [
        0.5 + sum((basis[coef_at] * params[11 + 3 * coef_at + channel] for coef_at in range(16)))
        for channel in range(3)
    ]
    log_opacity = params[10] - jnp.log1p(jnp.exp(params[10]))
    return [
        screen_u,
        screen_v,
        cov_c / determinant,
        -cov_b / determinant,
        cov_a / determinant,
        log_opacity,
        colors[0],
        colors[1],
        colors[2],
    ]


def both_halves(upper, lower):
    return jnp.concatenate([upper, lower], axis=0)


def camera_terms(cameras_ref, half):
    cameras = cameras_ref[...]
    cos, sin = jnp.cos(cameras), jnp.sin(cameras)

    def column(values, at):
        values = values[:, at : at + 1]
        return jnp.broadcast_to(both_halves(values, values), (KEYS, half))

    rotation = rotation_entries(
        [column(cos, at) for at in range(3)], [column(sin, at) for at in range(3)]
    )
    return rotation, [column(cameras, 3 + at) for at in range(3)]


def spread_params(params_ref, half):
    return [
        both_halves(
            jnp.broadcast_to(params_ref[at : at + 1, :half], (VIEWS, half)),
            jnp.broadcast_to(params_ref[at : at + 1, half:], (VIEWS, half)),
        )
        for at in range(PARAMS)
    ]


def iota(shape, dim):
    return lax.broadcasted_iota(i32, shape, dim)


def dot(left, right, left_dim, right_dim):
    return lax.dot_general(
        left, right, (((left_dim,), (right_dim,)), ((), ())), preferred_element_type=f32
    )


def halved_dot(left_ref, right_ref):
    half = left_ref.shape[1] // 2
    return dot(left_ref[:, :half], right_ref[:, :half], 1, 1) - dot(
        left_ref[:, half:], right_ref[:, half:], 1, 1
    )


def pieces(values, count):
    out = []
    for at in range(count):
        part = values.astype(bf16)
        out.append(part)
        if at + 1 < count:
            values = values - part.astype(f32)
    return out


def one_hot(ids, row):
    row = jnp.broadcast_to(row, (16, row.shape[1])).astype(bf16)
    row = jnp.concatenate([row] * (ids.shape[0] // 16), axis=0)
    return jnp.where(ids == row, jnp.ones((), bf16), jnp.zeros((), bf16))


def small_ids(count):
    return iota((count, LANES), 0).astype(f32).astype(bf16)


def rank_kernel(
    owned, lists_ref, entries_ref, rank_ref, request_ref, hot_ref, wanted_ref
):
    chunks = entries_ref.shape[0]
    per_group = chunks // 2
    steps = LANES // GROUP
    lane = iota((GROUP, LANES), 1)
    tile = lax.rem(lane, GROUP)
    spot = iota((GROUP, LANES), 0) * steps + lax.div(lane, GROUP)
    for group in range(2):
        for half in range(per_group // GROUP):
            made = jnp.zeros((GROUP, LANES), i32)
            for at in range(GROUP):
                row = group * GROUP + at
                source = jnp.broadcast_to(
                    lists_ref[row : row + 1, half * LANES : (half + 1) * LANES], (GROUP, LANES)
                )
                found = jnp.take_along_axis(source, spot, axis=1, mode="promise_in_bounds")
                made = jnp.where(tile == at, found, made)
            row = group * per_group + half * GROUP
            entries_ref[row : row + GROUP, :] = made
    entries = entries_ref[...]
    owner = lax.div(entries, owned)
    owner_row = owner.astype(f32)
    column = lax.rem(entries, owned)
    turn = jnp.where(iota(entries.shape, 0) < per_group, 1.0, -1.0)
    low = turn * lax.rem(column, 256).astype(f32)
    high = turn * lax.div(column, 256).astype(f32)
    before = jnp.where(iota((LANES, LANES), 0) < iota((LANES, LANES), 1), 1.0, 0.0)
    adder = jnp.concatenate([before, jnp.ones((LANES, LANES), f32)], axis=1).astype(bf16)
    owner_id = iota((LANES, LANES), 0)
    owner_one = small_ids(LANES)
    slot_one = small_ids(SLOTS)
    base = jnp.zeros((LANES, LANES), f32)
    for at in range(chunks):
        lanes = slice(at * LANES, (at + 1) * LANES)
        hot = one_hot(owner_one, owner_row[at : at + 1, :])
        hot_ref[:, lanes] = hot
        counts = dot(hot, adder, 1, 0)
        rank = jnp.sum(
            jnp.where(owner_id == owner[at : at + 1, :], counts[:, :LANES] + base, 0.0),
            axis=0,
            keepdims=True,
        )
        base = base + counts[:, LANES:]
        rank_ref[at : at + 1, :] = rank.astype(i32)
        slot = one_hot(slot_one, rank)
        wanted_ref[:, lanes] = jnp.concatenate(
            [
                slot * jnp.broadcast_to(part[at : at + 1, :], (SLOTS, LANES)).astype(bf16)
                for part in (low, high)
            ],
            axis=0,
        )
    requests = halved_dot(hot_ref, wanted_ref)
    request_ref[...] = requests[:, :SLOTS] + 256.0 * requests[:, SLOTS:]


def flipped_requests(asked_ref):
    asked = asked_ref[...]
    wide = jnp.concatenate([asked, jnp.zeros((LANES, LANES - SLOTS), f32)], axis=1)
    return wide.T[:SLOTS, :].astype(i32)


def project_kernel(frame, params_ref, cameras_ref, table_ref):
    half = params_ref.shape[1] // 2
    rotation, shift = camera_terms(cameras_ref, half)
    rows = project(spread_params(params_ref, half), rotation, shift, *frame)
    rows.append(jnp.zeros((TABLE - FEATURES * KEYS, half), f32))
    for part, values in enumerate(pieces(jnp.concatenate(rows, axis=0), 3)):
        table_ref[part * TABLE : (part + 1) * TABLE, :] = values


def request_keys(asked):
    half = 2 * LANES
    return lax.div(asked, half) * VIEWS + lax.div(iota(asked.shape, 1), LANES // VIEWS)


def spread_rows(stack, out_ref):
    for part in range(3):
        out_ref[pl.ds(part, LANES, stride=3), :] = stack[part * LANES : (part + 1) * LANES].T


def gathered_rows(rows_ref):
    return jnp.concatenate(
        [rows_ref[pl.ds(part, LANES, stride=3), :].T for part in range(3)], axis=0
    )


def pick_sublane(values, row):
    index = jnp.broadcast_to(row, (8, values.shape[1]))
    return jnp.take_along_axis(values, index, axis=0, mode="promise_in_bounds")


def fill_columns(asked, column_ref):
    low = lax.rem(asked, 2 * LANES).astype(f32)
    ids = small_ids(2 * LANES)
    for at in range(SLOTS):
        column_ref[:, at * LANES : (at + 1) * LANES] = one_hot(ids, low[at : at + 1, :])


def answer_kernel(table_ref, asked_ref, rows_ref, column_ref, stack_ref):
    asked = flipped_requests(asked_ref)
    key = request_keys(asked)
    fill_columns(asked, column_ref)
    table = table_ref[...]
    for at in range(0, SLOTS, 2):
        found = dot(table, column_ref[:, at * LANES : (at + 2) * LANES], 1, 0)
        found = found[:TABLE] + (found[TABLE : 2 * TABLE] + found[2 * TABLE :])
        for side in range(2):
            slot = at + side
            for feature in range(FEATURES):
                row = slot // HALF * FEATURES * HALF + feature * HALF + slot % HALF
                stack_ref[row : row + 1, :] = pick_sublane(
                    found[feature * KEYS : (feature + 1) * KEYS, side * LANES : (side + 1) * LANES],
                    key[slot : slot + 1, :],
                )[:1, :]
    stack_ref[SLOTS * FEATURES :, :] = jnp.zeros((3 * LANES - SLOTS * FEATURES, LANES), f32)
    spread_rows(stack_ref[...], rows_ref)


def prepare_kernel(
    owned,
    entries_ref,
    rank_ref,
    lengths_ref,
    target_ref,
    first_ref,
    second_ref,
    hot_ref,
    live_ref,
    aim_ref,
    old_first_ref,
    old_second_ref,
):
    old_first_ref[...] = beta_one * first_ref[...]
    old_second_ref[...] = beta_two * second_ref[...]
    ids = small_ids(2 * LANES)
    place, _ = slot_columns(entries_ref[...], rank_ref[...], owned)
    place = place.astype(f32)
    for at in range(entries_ref.shape[0]):
        hot_ref[:, at * LANES : (at + 1) * LANES] = one_hot(ids, place[at : at + 1, :])
    lengths = jnp.concatenate(
        [lengths_ref[...], jnp.zeros((1, LANES - lengths_ref.shape[1]), i32)], axis=1
    )
    shape = entries_ref.shape
    per_group = shape[0] // 2
    tile = lax.div(iota(shape, 0), per_group) * GROUP + lax.rem(iota(shape, 1), GROUP)
    length = jnp.take_along_axis(
        jnp.broadcast_to(lengths, shape), tile, axis=1, mode="promise_in_bounds"
    )
    steps = LANES // GROUP
    spot = lax.rem(iota(shape, 0), per_group) * steps + lax.div(iota(shape, 1), GROUP)
    live_ref[...] = jnp.where(spot < length, 1, 0)
    aim_ref[...] = target_ref[...]


def slot_columns(entries, rank, owned):
    owner = lax.div(entries, owned)
    return lax.div(rank, HALF) * LANES + owner, lax.rem(rank, HALF)


def tile_kernel(
    live_ref,
    rank_ref,
    hot_ref,
    rows_ref,
    target_ref,
    grads_ref,
    picked_ref,
    coef_ref,
    color_ref,
    alpha_ref,
    weight_ref,
    high_ref,
    middle_ref,
    low_ref,
    pull_ref,
    moment_ref,
    grad_ref,
    spread_ref,
    paint_ref,
):
    chunks = live_ref.shape[0]
    groups = 2
    per_group = chunks // groups
    pixels = TILE_SIDE * TILE_SIDE
    steps = LANES // GROUP
    span = FEATURES * HALF
    first_tile = lax.axis_index("tiles") * (groups * GROUP)

    live = live_ref[...] > 0
    below = lax.rem(rank_ref[...], HALF)

    flipped = gathered_rows(rows_ref)
    table = jnp.concatenate([flipped[:span], flipped[span : 2 * span]], axis=1)
    table = jnp.concatenate(pieces(table, 3), axis=0)
    for at in range(0, chunks, 2):
        found = dot(table, hot_ref[:, at * LANES : (at + 2) * LANES], 1, 0)
        found = found[:span] + (found[span : 2 * span] + found[2 * span :])
        for side in range(2):
            row = below[at + side : at + side + 1, :]
            index, upper = lax.rem(row, 8), jnp.broadcast_to(row, (8, LANES)) >= 8
            for feature in range(FEATURES):
                first, second = [
                    pick_sublane(
                        found[part : part + 8, side * LANES : (side + 1) * LANES], index
                    )
                    for part in (feature * HALF, feature * HALF + 8)
                ]
                row = feature * chunks + at + side
                picked_ref[row : row + 1, :] = jnp.where(upper, second, first)[:1, :]
    shape = (chunks, LANES)
    chosen = [picked_ref[at * chunks : (at + 1) * chunks, :] for at in range(FEATURES)]

    tile = first_tile + lax.div(iota(shape, 0), per_group) * GROUP + lax.rem(iota(shape, 1), GROUP)
    middle_x = (lax.rem(tile, TILE_COLS) * TILE_SIDE + TILE_SIDE // 2).astype(f32)
    middle_y = (lax.div(tile, TILE_COLS) * TILE_SIDE + TILE_SIDE // 2).astype(f32)
    at_u = chosen[0] - middle_x
    at_v = chosen[1] - middle_y
    conic_a, conic_b, conic_c = chosen[2], chosen[3], chosen[4]
    by_u = conic_a * at_u + conic_b * at_v
    by_v = conic_b * at_u + conic_c * at_v
    coefs = [
        jnp.where(live, log2_e * (chosen[5] - 0.5 * (at_u * by_u + at_v * by_v)), -1e4),
        jnp.where(live, log2_e * by_u, 0.0),
        jnp.where(live, log2_e * by_v, 0.0),
        jnp.where(live, (-0.5 * log2_e) * conic_a, 0.0),
        jnp.where(live, -log2_e * conic_b, 0.0),
        jnp.where(live, (-0.5 * log2_e) * conic_c, 0.0),
    ]
    for at in range(8):
        split = pieces(coefs[at], 3) if at < 6 else [jnp.zeros(shape, bf16)] * 3
        for part in range(3):
            row = (part * 8 + at) * chunks
            coef_ref[row : row + chunks, :] = split[part].astype(f32)
    for at in range(3):
        split = pieces(chosen[6 + at], 3)
        for part in range(3):
            row = (part * 3 + at) * chunks
            color_ref[row : row + chunks, :] = split[part].astype(f32)

    pixel = iota((8, pixels), 1)
    row8 = iota((8, pixels), 0)
    off_x = lax.rem(pixel, TILE_SIDE).astype(f32) - 7.5
    off_y = lax.div(pixel, TILE_SIDE).astype(f32) - 7.5
    base = jnp.where(row8 == 0, 1.0, 0.0)
    for at, values in enumerate([off_x, off_y, off_x * off_x, off_x * off_y, off_y * off_y]):
        base = jnp.where(row8 == at + 1, values, base)
    base_two = jnp.concatenate([base, base], axis=1).astype(bf16)
    base_three = jnp.concatenate([base, base, base], axis=0).astype(bf16)
    same_tile = lax.rem(iota((GROUP, LANES), 1), GROUP) == iota((GROUP, LANES), 0)

    for at in range(chunks):
        rows = []
        for part in range(9):
            row = color_ref[part * chunks + at : part * chunks + at + 1, :]
            rows.append(jnp.where(same_tile, jnp.broadcast_to(row, (GROUP, LANES)), 0.0))
        rows.append(jnp.zeros((GROUP, LANES), f32))
        paint_ref[:, at * LANES : (at + 1) * LANES] = jnp.concatenate(rows, axis=0).astype(bf16)

    def rows_of(chunk, count=1):
        return slice(chunk * LANES, (chunk + count) * LANES)

    def shade(first, count):
        for group in range(groups):
            chunk = group * per_group + first
            coef = jnp.concatenate(
                [coef_ref[pl.ds(chunk + off, 24, stride=chunks), :] for off in range(count)], axis=1
            )
            alpha_ref[rows_of(chunk, count), :] = jnp.exp2(
                dot(coef.astype(bf16), base_three, 0, 0)
            )

    def pairs_of(at, group):
        start = (group * per_group + at) * LANES
        return [slice(start + off, start + off + 2 * GROUP) for off in range(0, LANES, 2 * GROUP)]

    def weigh(at, clears):
        clears = list(clears)
        for pair in range(steps // 2):
            for group in range(groups):
                rows = pairs_of(at, group)[pair]
                alpha = alpha_ref[rows, :]
                weights = []
                for part in (alpha[:GROUP], alpha[GROUP:]):
                    weights.append(part * clears[group])
                    clears[group] = clears[group] - weights[-1]
                weight = jnp.concatenate(weights, axis=0)
                weight_ref[rows, :] = weight
                high_ref[rows, :], middle_ref[rows, :], low_ref[rows, :] = pieces(weight, 3)
        return tuple(clears)

    def blend(first, count, renders):
        out = []
        for group in range(groups):
            rows = rows_of(group * per_group + first, count)
            paint = paint_ref[:72, rows]
            out.append(
                renders[group]
                + (
                    dot(paint, high_ref[rows, :], 1, 0)
                    + (dot(paint, middle_ref[rows, :], 1, 0) + dot(paint, low_ref[rows, :], 1, 0))
                )
            )
        return tuple(out)

    clears = (jnp.ones((GROUP, pixels), f32),) * groups
    renders = (jnp.zeros((72, pixels), f32),) * groups
    shade(*BLOCKS[0])
    for block, (first, count) in enumerate(BLOCKS):
        if block + 1 < len(BLOCKS):
            shade(*BLOCKS[block + 1])
        for at in range(first, first + count):
            clears = weigh(at, clears)
        renders = blend(first, count, renders)

    signs, sign_twos = [], []
    for group in range(groups):
        render = renders[group]
        render = render[:24] + (render[24:48] + render[48:])
        rows = []
        for at in range(3):
            gap = (
                render[at * GROUP : (at + 1) * GROUP, :]
                - target_ref[at, group * GROUP : (group + 1) * GROUP, :]
            )
            rows.append(jnp.where(gap > 0.0, 1.0, jnp.where(gap < 0.0, -1.0, 0.0)))
        sign = jnp.concatenate(rows, axis=0)
        signs.append(sign.astype(bf16))
        sign_twos.append(jnp.concatenate([sign, sign], axis=0).astype(bf16))

    def draw(first, count):
        for group in range(groups):
            rows = rows_of(group * per_group + first, count)
            pull_ref[rows, :] = dot(paint_ref[:48, rows], sign_twos[group], 0, 0)

    def unweigh(at, behinds):
        behinds = list(behinds)
        for pair in reversed(range(steps // 2)):
            for group in range(groups):
                rows = pairs_of(at, group)[pair]
                pull, alpha, weight = pull_ref[rows, :], alpha_ref[rows, :], weight_ref[rows, :]
                by_alpha = []
                for part in (slice(GROUP, 2 * GROUP), slice(0, GROUP)):
                    gap = pull[part] - behinds[group]
                    by_alpha.insert(0, weight[part] * gap)
                    behinds[group] = behinds[group] + alpha[part] * gap
                low_ref[rows, :], spread_ref[rows, :] = pieces(jnp.concatenate(by_alpha, axis=0), 2)
        return tuple(behinds)

    def total(first, count):
        for group in range(groups):
            chunk = group * per_group + first
            rows = rows_of(chunk, count)
            parts = jnp.concatenate([low_ref[rows, :], spread_ref[rows, :]], axis=1)
            moments = dot(base_two, parts, 1, 1)
            by_color = dot(signs[group], high_ref[rows, :], 1, 1)
            for off in range(count):
                row = (chunk + off) * 16
                lanes = slice(off * LANES, (off + 1) * LANES)
                moment_ref[pl.ds(row, 8), :] = moments[:, lanes]
                for channel in range(3):
                    moment_ref[pl.ds(row + 8 + channel, 1), :] = jnp.sum(
                        jnp.where(
                            same_tile, by_color[channel * GROUP : (channel + 1) * GROUP, lanes], 0.0
                        ),
                        axis=0,
                        keepdims=True,
                    )

    behinds = (jnp.zeros((GROUP, pixels), f32),) * groups
    draw(*BLOCKS[-1])
    for block in reversed(range(len(BLOCKS))):
        if block:
            draw(*BLOCKS[block - 1])
        first, count = BLOCKS[block]
        for at in reversed(range(first, first + count)):
            behinds = unweigh(at, behinds)
        total(first, count)

    sums = [moment_ref[pl.ds(at, chunks, stride=16), :] for at in range(6)]
    sum_x = sums[1] - at_u * sums[0]
    sum_y = sums[2] - at_v * sums[0]
    sum_xx = sums[3] - 2.0 * at_u * sums[1] + at_u * at_u * sums[0]
    sum_xy = sums[4] - at_u * sums[2] - at_v * sum_x
    sum_yy = sums[5] - 2.0 * at_v * sums[2] + at_v * at_v * sums[0]
    grads = [
        conic_a * sum_x + conic_b * sum_y,
        conic_b * sum_x + conic_c * sum_y,
        -0.5 * sum_xx,
        -sum_xy,
        -0.5 * sum_yy,
        sums[0],
    ] + [moment_ref[pl.ds(8 + at, chunks, stride=16), :] for at in range(3)]

    half_one = small_ids(HALF)
    below = below.astype(f32)
    turn = jnp.where(live, jnp.where(iota(shape, 0) < per_group, 1.0, -1.0), 0.0)
    grads = [pieces(turn * grad, 2) for grad in grads]
    grads = [[part.astype(f32) for part in split] for split in grads]
    for at in range(chunks):
        mask = one_hot(half_one, below[at : at + 1, :])
        for part in range(2):
            for feature in range(FEATURES):
                row = grads[feature][part][at : at + 1, :]
                grad_ref[
                    part * span + feature * HALF : part * span + (feature + 1) * HALF,
                    at * LANES : (at + 1) * LANES,
                ] = mask * jnp.broadcast_to(row, (HALF, LANES)).astype(bf16)
    sent = halved_dot(grad_ref, hot_ref)
    sent = sent[:span] + sent[span:]
    sent = jnp.concatenate(
        [sent[:, :LANES], sent[:, LANES:], jnp.zeros((3 * LANES - 2 * span, LANES), f32)], axis=0
    )
    spread_rows(sent, grads_ref)


def tiles_call(live, rank, hot, rows, target):
    chunks = live.shape[0]
    pixels = TILE_SIDE * TILE_SIDE
    count = chunks * LANES

    def plane(dtype):
        return pltpu.VMEM((count, pixels), dtype)

    return pl.pallas_call(
        tile_kernel,
        out_shape=jax.ShapeDtypeStruct((3 * LANES, LANES), f32),
        scratch_shapes=[
            pltpu.VMEM((FEATURES * chunks, LANES), f32),
            pltpu.VMEM((24 * chunks, LANES), f32),
            pltpu.VMEM((9 * chunks, LANES), f32),
            plane(f32),
            plane(f32),
            plane(bf16),
            plane(bf16),
            plane(bf16),
            plane(f32),
            pltpu.VMEM((16 * chunks, LANES), f32),
            pltpu.VMEM((2 * FEATURES * HALF, count), bf16),
            plane(bf16),
            pltpu.VMEM((80, count), bf16),
        ],
        compiler_params=pltpu.CompilerParams(vmem_limit_bytes=32 * 1024 * 1024),
        name="tiles",
    )(live, rank, hot, rows, target)


def learning_rates(shape):
    row = iota(shape, 0)
    rates = jnp.full(shape, 0.000125, f32)
    for stop, rate in ((14, 0.0025), (11, 0.05), (10, 0.001), (6, 0.005), (3, 0.00016)):
        rates = jnp.where(row < stop, rate, rates)
    return rates


def update_kernel(
    frame,
    params_ref,
    old_first_ref,
    old_second_ref,
    cameras_ref,
    asked_ref,
    grads_ref,
    new_params_ref,
    new_first_ref,
    new_second_ref,
    source_ref,
    spread_ref,
    column_ref,
    gradient_ref,
):
    owned = params_ref.shape[1]
    half = owned // 2
    asked = flipped_requests(asked_ref)
    key = request_keys(asked)
    fill_columns(asked, column_ref)
    flipped = gathered_rows(grads_ref)
    first_half = iota(flipped.shape, 0) < FEATURES * HALF
    for part, values in enumerate(pieces(flipped, 2)):
        values = values.astype(f32)
        source_ref[part * 3 * LANES : (part + 1) * 3 * LANES, :] = jnp.where(first_half, values, -values)
    key_id = iota((KEYS, LANES), 0)
    for slot in range(SLOTS):
        first = slot // HALF * FEATURES * HALF + slot % HALF
        mine = key_id == key[slot : slot + 1, :]
        rows = []
        for part in range(2):
            for feature in range(FEATURES):
                at = part * 3 * LANES + first + feature * HALF
                row = jnp.broadcast_to(source_ref[at : at + 1, :], (KEYS, LANES))
                rows.append(jnp.where(mine, row, 0.0))
        spread_ref[:, slot * LANES : (slot + 1) * LANES] = jnp.concatenate(rows, axis=0).astype(bf16)
    dense = halved_dot(spread_ref, column_ref)
    dense = dense[: FEATURES * KEYS] + dense[FEATURES * KEYS :]
    cotangents = [dense[at * KEYS : (at + 1) * KEYS] for at in range(FEATURES)]

    rotation, shift = camera_terms(cameras_ref, half)
    params = spread_params(params_ref, half)
    _, pullback = jax.vjp(lambda values: project(values, rotation, shift, *frame), params)
    by_params = pullback(cotangents)[0]
    for at in range(PARAMS):
        pair = by_params[at] + pltpu.roll(by_params[at], 1, 0)
        four = pair + pltpu.roll(pair, 2, 0)
        gradient_ref[at : at + 1, :half] = four[VIEWS - 1 : VIEWS]
        gradient_ref[at : at + 1, half:] = four[KEYS - 1 :]
    gradient = gradient_ref[:PARAMS, :]
    new_first = old_first_ref[...] + (1.0 - beta_one) * gradient
    new_second = old_second_ref[...] + (1.0 - beta_two) * gradient * gradient
    new_first_ref[...] = new_first
    new_second_ref[...] = new_second
    step_size = learning_rates((PARAMS, owned)) * (new_first / (1.0 - beta_one**ADAM_STEP))
    new_params_ref[...] = params_ref[...] - step_size / (
        jnp.sqrt(new_second / (1.0 - beta_two**ADAM_STEP)) + adam_eps
    )


def per_device(params, first_moment, second_moment, cameras, target, lists, lengths):
    owned = params.shape[1]
    list_size = lists.shape[2]
    tile_dev = lists.shape[1]
    entry_count = tile_dev * list_size
    chunks = entry_count // LANES
    width = TILE_COLS * TILE_SIDE
    height = tile_dev * lax.axis_size("tiles") // TILE_COLS * TILE_SIDE
    frame = (float(width), 0.5 * width, 0.5 * height)
    limits = pltpu.CompilerParams(vmem_limit_bytes=16 * 1024 * 1024)

    def full(shape, dtype=f32):
        return jax.ShapeDtypeStruct(shape, dtype)

    def sent(rows):
        rows = lax.all_to_all(rows.reshape(LANES, 3 * LANES), AXES, 0, 0, tiled=True)
        return rows.reshape(3 * LANES, LANES)

    entries, rank, requests = pl.pallas_call(
        lambda *refs: rank_kernel(owned, *refs),
        out_shape=(full((chunks, LANES), i32), full((chunks, LANES), i32), full((LANES, SLOTS))),
        scratch_shapes=[
            pltpu.VMEM((LANES, entry_count), bf16),
            pltpu.VMEM((2 * SLOTS, entry_count), bf16),
        ],
        compiler_params=limits,
        name="rank",
    )(lists[0])
    asked = lax.all_to_all(requests, AXES, 0, 0, tiled=True)
    table = pl.pallas_call(
        lambda *refs: project_kernel(frame, *refs),
        out_shape=full((3 * TABLE, owned // 2), bf16),
        compiler_params=limits,
        cost_estimate=pl.CostEstimate(flops=4000000, bytes_accessed=200000, transcendentals=20000),
        name="project",
    )(params, cameras)
    columns = (owned // 2, SLOTS * LANES)
    answers = pl.pallas_call(
        answer_kernel,
        out_shape=full((3 * LANES, LANES)),
        scratch_shapes=[pltpu.VMEM(columns, bf16), pltpu.VMEM((3 * LANES, LANES), f32)],
        compiler_params=limits,
        name="answer",
    )(table, asked)
    rows = sent(answers)
    aim = target[0].transpose(1, 0, 2)
    hot, live, aim, old_first, old_second = pl.pallas_call(
        lambda *refs: prepare_kernel(owned, *refs),
        out_shape=(
            full((2 * LANES, entry_count), bf16),
            full((chunks, LANES), i32),
            full(aim.shape),
            full(params.shape),
            full(params.shape),
        ),
        compiler_params=limits,
        cost_estimate=pl.CostEstimate(flops=4000000, bytes_accessed=2200000, transcendentals=0),
        name="prepare",
    )(entries, rank, lengths, aim, first_moment, second_moment)
    row_grads = tiles_call(live, rank, hot, rows, aim)
    shares = sent(row_grads)
    return pl.pallas_call(
        lambda *refs: update_kernel(frame, *refs),
        out_shape=(full(params.shape),) * 3,
        scratch_shapes=[
            pltpu.VMEM((6 * LANES, LANES), f32),
            pltpu.VMEM((2 * FEATURES * KEYS, SLOTS * LANES), bf16),
            pltpu.VMEM(columns, bf16),
            pltpu.VMEM((64, owned), f32),
        ],
        compiler_params=limits,
        name="update",
    )(params, old_first, old_second, cameras, asked, shares)


def solution(mesh):
    placed = (
        P(None, AXES),
        P(None, AXES),
        P(None, AXES),
        P(),
        P("views", "tiles", None, None),
        P("views", "tiles", None),
        P("views", "tiles"),
    )
    return jax.shard_map(
        per_device,
        mesh=mesh,
        in_specs=placed,
        out_specs=(P(None, AXES),) * 3,
        check_vma=False,
    )
```
